32 devices in a mesh: blk: 16 (over z, x, core), fsdp: 2 (over y).
Axes of the slice: x: 2, y: 2, z: 4, core: 2. Of those that a mesh axis runs over, the one named last changes fastest.
Arguments:
- params: float32 [16, 4096, 1024], P('blk', 'fsdp'), may hold values from -6 to 6
- inputs: bfloat16 [16, 1792, 4096], P('blk', 'fsdp'), may hold values from -6 to 6
- cotangent: bfloat16 [16, 1792, 1024], P('blk', 'fsdp'), may hold values from -6 to 6
- mix: int32 [16, 3], replicated, may hold values from 8 to 48, as said below
Outputs:
- new_params: float32 [16, 4096, 1024], P('blk', 'fsdp')
The draws below stay inside these ranges and needn't reach their ends.
Inputs may be any that keep to these rules, and one draw needn't show every extreme that they name: `mix`: each row holds three positive numerators that sum to 64.
All inputs are finite; a program needn't handle non-finite values.
Results may differ from the reference program's by a relative error of at most 0.0003.
Values may be sent and summed in bfloat16 or wider, within the bound.
No kernel may reach another device: no remote copies, remote signals or barrier semaphores. Data moves between devices by JAX's collectives and lax.ppermute only.
A program may use at most 128 MiB of HBM per device.

```python
import jax
import jax.numpy as jnp
from jax import lax

D = 4096
KV = 1024
TOK_DEV = 896
MIX_DENOM = 64
TOKENS = 1792
NREP = 16
N_FSDP = 2


def draw_mix(key, part):
    key_left, key_right = jax.random.split(jax.random.fold_in(key, 17))
    left_part = jax.random.randint(key_left, (NREP, 1), 8, 25)
    right_part = jax.random.randint(key_right, (NREP, 1), 8, 25)
    return jnp.concatenate([left_part, MIX_DENOM - left_part - right_part, right_part], axis=1).astype(jnp.int32)


def block_levels(rng, extent, cuts, least, top_value):
    def one(dim, blocks):
        draws = jax.random.uniform(jax.random.fold_in(jax.random.fold_in(rng, 6), dim), (blocks,), jnp.float32, least / len(cuts), top_value / len(cuts))
        return jnp.repeat(jnp.exp(draws), extent[dim] // blocks).reshape((-1,) + (1,) * (len(extent) - dim - 1))

    gain = one(*cuts[0])
    for cut in cuts[1:]:
        gain = gain * one(*cut)
    return gain


def scatter_about(key, dims, scale, most, pieces=(), kind=jnp.bfloat16):
    drawn = jax.random.normal(key, dims, jnp.float32) * scale
    if len(pieces) > 0:
        drawn = block_levels(key, dims, pieces, -0.22, 0.18) * drawn
    return jnp.clip(drawn, min=-most, max=most).astype(kind)


def setup_inputs(seed: int = 0) -> dict:
    keys = jax.random.split(jax.random.key(seed), 5)
    params = scatter_about(keys[0], (NREP, D, KV), 1.0, 6.0, ((0, 16), (1, 2)), jnp.float32)
    inputs = scatter_about(keys[1], (NREP, TOKENS, D), 1.0, 6.0, ((0, 16), (1, 2)))
    cotangent = scatter_about(keys[2], (NREP, TOKENS, KV), 1.0, 6.0, ((0, 16), (1, 2)))
    mix = draw_mix(jax.random.fold_in(keys[4], 71), 0)
    return dict(params=params, inputs=inputs, cotangent=cotangent, mix=mix)


RATE = 0.03

def replica_grad(pair):
    inputs_r, cot_r = pair
    x_blocks = inputs_r.reshape(N_FSDP, TOK_DEV, D)
    c_blocks = cot_r.reshape(N_FSDP, TOK_DEV, KV)

    def add_block(total, blocks):
        x_block, c_block = blocks
        part = jnp.dot(x_block.T, c_block, preferred_element_type=jnp.float32)
        return (total + part, None)
    total, unused = lax.scan(add_block, jnp.zeros((D, KV), jnp.float32), (x_blocks, c_blocks))
    return total

def reference(params, inputs, cotangent, mix):
    gradient = lax.map(replica_grad, (inputs, cotangent))
    coeff = mix.astype(jnp.float32) / MIX_DENOM
    c_left = coeff[:, 0][:, None, None]
    c_self = coeff[:, 1][:, None, None]
    c_right = coeff[:, 2][:, None, None]
    mixed_params = c_left * jnp.roll(params, 1, 0) + c_self * params + c_right * jnp.roll(params, -1, 0)
    mixed_grads = c_left * jnp.roll(gradient, 1, 0) + c_self * gradient + c_right * jnp.roll(gradient, -1, 0)
    return mixed_params - RATE * mixed_grads
```

```python
import math

import jax
import jax.numpy as jnp
from jax import lax
from jax.sharding import PartitionSpec as P

MIX_DENOM = 64
RATE = 0.03
LARGEST = 6.0
WIRE = jnp.float16
CHUNKS = 8
AHEAD = 2
LAG = 2


def from_behind(value, axis, steps):
    count = lax.axis_size(axis)
    pairs = [(source, (source + steps) % count) for source in range(count)]
    return lax.ppermute(value, axis, pairs)


def wire_scale(tokens):
    bound = LARGEST + RATE * LARGEST * LARGEST * tokens
    return 2.0 ** math.floor(math.log2(float(jnp.finfo(WIRE).max) / bound))


def on_device(params, inputs, cotangent, mix):
    weights = params[0]
    features = inputs[0]
    cot_local = cotangent[0]
    rows = weights.shape[0]
    shards = lax.axis_size("fsdp")
    scale = wire_scale(features.shape[0] * shards)
    replica = lax.axis_index("blk")
    shard = lax.axis_index("fsdp")
    pick = (jnp.arange(lax.axis_size("blk")) == replica).astype(jnp.float32)
    coeff = jnp.dot(pick, mix.astype(jnp.float32), precision=lax.Precision.HIGHEST) / MIX_DENOM
    c_left = coeff[0] / scale
    c_self = coeff[1]
    c_right = coeff[2] / scale
    step = rows // CHUNKS

    def partial(owner, chunk):
        block = lax.dynamic_slice_in_dim(features, owner * rows + chunk * step, step, axis=1)
        return lax.dot_general(
            block, cot_local, (((0,), (0,)), ((), ())), preferred_element_type=jnp.float32
        )

    def others(chunk):
        return [
            (partial(lax.rem(shard + away, shards), chunk) * (RATE * scale)).astype(WIRE)
            for away in range(1, shards)
        ]

    arrived = {}
    mine = {}
    sides = {}
    out = jnp.zeros_like(weights)

    def send_terms(chunk):
        terms = others(chunk)
        if chunk >= AHEAD:
            terms, arrived[chunk - AHEAD] = lax.optimization_barrier((terms, arrived[chunk - AHEAD]))
        arrived[chunk] = [
            from_behind(term, "fsdp", away) for away, term in zip(range(1, shards), terms)
        ]

    def finish(chunk, out):
        left, right = sides[chunk]
        mixed = c_left * left.astype(jnp.float32) + c_self * mine[chunk] + c_right * right.astype(jnp.float32)
        return lax.dynamic_update_slice_in_dim(out, mixed, chunk * step, axis=0)

    for chunk in range(AHEAD):
        send_terms(chunk)
    for chunk in range(CHUNKS):
        if chunk + AHEAD < CHUNKS:
            send_terms(chunk + AHEAD)
        before = weights[chunk * step:(chunk + 1) * step]
        total = partial(shard, chunk)
        if chunk >= 1:
            before, total, sent = lax.optimization_barrier((before, total, sent))
        total = RATE * total
        for term in arrived[chunk]:
            total = total + term.astype(jnp.float32) / scale
        own = before - total
        mine[chunk], sent = lax.optimization_barrier((own, (own * scale).astype(WIRE)))
        sides[chunk] = (from_behind(sent, "blk", 1), from_behind(sent, "blk", -1))
        if chunk >= LAG:
            sides[chunk - LAG], mine[chunk] = lax.optimization_barrier((sides[chunk - LAG], mine[chunk]))
            out = finish(chunk - LAG, out)
    for chunk in range(CHUNKS - LAG, CHUNKS):
        out = finish(chunk, out)
    return out[None]


def solution(mesh):
    return jax.shard_map(
        on_device,
        mesh=mesh,
        in_specs=(P("blk", "fsdp", None), P("blk", "fsdp", None), P("blk", "fsdp", None), P()),
        out_specs=P("blk", "fsdp", None),
        check_vma=False,
    )
```

```python
import math

import jax
import jax.numpy as jnp
from jax import lax
from jax.sharding import PartitionSpec as P

MIX_DENOM = 64
RATE = 0.03
LARGEST = 6.0
WIRE = jnp.float16
CHUNKS = 8
AHEAD = 2


def from_behind(value, axis, steps):
    count = lax.axis_size(axis)
    pairs = [(source, (source + steps) % count) for source in range(count)]
    return lax.ppermute(value, axis, pairs)


def swapped(value, axis, first):
    count = lax.axis_size(axis)
    pairs = []
    for source in range(first, count, 2):
        partner = (source + 1) % count
        pairs += [(source, partner), (partner, source)]
    return lax.ppermute(value, axis, pairs)


def wire_scale(tokens):
    bound = LARGEST + RATE * LARGEST * LARGEST * tokens
    return 2.0 ** math.floor(math.log2(float(jnp.finfo(WIRE).max) / bound))


def on_device(params, inputs, cotangent, mix):
    weights = params[0]
    features = inputs[0]
    cot_local = cotangent[0]
    rows = weights.shape[0]
    shards = lax.axis_size("fsdp")
    scale = wire_scale(features.shape[0] * shards)
    replica = lax.axis_index("blk")
    shard = lax.axis_index("fsdp")
    pick = (jnp.arange(lax.axis_size("blk")) == replica).astype(jnp.float32)
    coeff = jnp.dot(pick, mix.astype(jnp.float32), precision=lax.Precision.HIGHEST) / MIX_DENOM
    even = replica % 2 == 0
    c_self = coeff[1]
    c_near = jnp.where(even, coeff[2], coeff[0]) / scale
    c_far = jnp.where(even, coeff[0], coeff[2]) / scale
    step = rows // CHUNKS

    def partial(owner, first, count):
        block = lax.dynamic_slice_in_dim(features, owner * rows + first, count, axis=1)
        return lax.dot_general(
            block, cot_local, (((0,), (0,)), ((), ())), preferred_element_type=jnp.float32
        )

    def for_others(first, count):
        return [
            (partial(lax.rem(shard + away, shards), first, count) * (RATE * scale)).astype(WIRE)
            for away in range(1, shards)
        ]

    def send_terms(terms):
        return [from_behind(term, "fsdp", away) for away, term in zip(range(1, shards), terms)]

    def rows_of(value, chunk):
        return value[chunk * step:(chunk + 1) * step]

    terms = {chunk: for_others(chunk * step, step) for chunk in range(AHEAD)}
    arrived = {chunk: send_terms(terms[chunk]) for chunk in range(AHEAD)}
    gradient = partial(shard, 0, rows)
    rest = for_others(AHEAD * step, rows - AHEAD * step)
    mine = {}
    near = {}
    far = {}
    out = jnp.zeros_like(weights)

    def finish(chunk, out):
        mixed = (
            c_near * near[chunk].astype(jnp.float32)
            + c_self * mine[chunk]
            + c_far * far[chunk].astype(jnp.float32)
        )
        return lax.dynamic_update_slice_in_dim(out, mixed, chunk * step, axis=0)

    for chunk in range(CHUNKS):
        if chunk >= 1:
            arrived[chunk], mine[chunk - 1], out = lax.optimization_barrier(
                (arrived[chunk], mine[chunk - 1], out)
            )
        total = RATE * rows_of(gradient, chunk)
        for term in arrived[chunk]:
            total = total + term.astype(jnp.float32) / scale
        own = rows_of(weights, chunk) - total
        mine[chunk], sent = lax.optimization_barrier((own, (own * scale).astype(WIRE)))
        if chunk + AHEAD < CHUNKS:
            rest, sent = lax.optimization_barrier((rest, sent))
            arrived[chunk + AHEAD] = send_terms([rows_of(term, chunk) for term in rest])
        far[chunk] = swapped(sent, "blk", 1)
        near[chunk] = swapped(sent, "blk", 0)
        if chunk >= 1:
            out = finish(chunk - 1, out)
    out = finish(CHUNKS - 1, out)
    return out[None]


def solution(mesh):
    return jax.shard_map(
        on_device,
        mesh=mesh,
        in_specs=(P("blk", "fsdp", None), P("blk", "fsdp", None), P("blk", "fsdp", None), P()),
        out_specs=P("blk", "fsdp", None),
        check_vma=False,
    )
```

```python
import math

import jax
import jax.numpy as jnp
from jax import lax
from jax.sharding import PartitionSpec as P

MIX_DENOM = 64
RATE = 0.03
LARGEST = 6.0
WIRE = jnp.float16
CHUNKS = 8
AHEAD = 2


def from_behind(value, axis, steps):
    count = lax.axis_size(axis)
    pairs = [(source, (source + steps) % count) for source in range(count)]
    return lax.ppermute(value, axis, pairs)


def swapped(value, axis, first):
    count = lax.axis_size(axis)
    pairs = []
    for source in range(first, count, 2):
        partner = (source + 1) % count
        pairs += [(source, partner), (partner, source)]
    return lax.ppermute(value, axis, pairs)


def wire_scale(tokens):
    bound = LARGEST + RATE * LARGEST * LARGEST * tokens
    return 2.0 ** math.floor(math.log2(float(jnp.finfo(WIRE).max) / bound))


def on_device(params, inputs, cotangent, mix):
    weights = params[0]
    features = inputs[0]
    cot_local = cotangent[0]
    rows = weights.shape[0]
    shards = lax.axis_size("fsdp")
    scale = wire_scale(features.shape[0] * shards)
    replica = lax.axis_index("blk")
    shard = lax.axis_index("fsdp")
    pick = (jnp.arange(lax.axis_size("blk")) == replica).astype(jnp.float32)
    coeff = jnp.dot(pick, mix.astype(jnp.float32), precision=lax.Precision.HIGHEST) / MIX_DENOM
    even = replica % 2 == 0
    c_self = coeff[1]
    c_near = jnp.where(even, coeff[2], coeff[0]) / scale
    c_far = jnp.where(even, coeff[0], coeff[2]) / scale
    step = rows // CHUNKS

    def partial(owner, first, count):
        block = lax.dynamic_slice_in_dim(features, owner * rows + first, count, axis=1)
        return lax.dot_general(
            block, cot_local, (((0,), (0,)), ((), ())), preferred_element_type=jnp.float32
        )

    def for_others(shard, first, count):
        return [
            (partial(lax.rem(shard + away, shards), first, count) * (RATE * scale)).astype(WIRE)
            for away in range(1, shards)
        ]

    def send_terms(terms):
        return [from_behind(term, "fsdp", away) for away, term in zip(range(1, shards), terms)]

    def rows_of(value, chunk):
        return value[chunk * step:(chunk + 1) * step]

    arrived = {}
    for chunk in range(AHEAD):
        arrived[chunk] = send_terms(for_others(shard, chunk * step, step))
    first = AHEAD * step
    gradient = {"first": partial(shard, 0, first)}
    rest = for_others(shard, first, rows - first)
    terms = {
        chunk: [rows_of(term, chunk - AHEAD) for term in rest] for chunk in range(AHEAD, CHUNKS)
    }
    mine = {}
    near = {}
    far = {}

    arrived[0], terms, gradient = lax.optimization_barrier((arrived[0], terms, gradient))
    for chunk in range(CHUNKS):
        if chunk == 1:
            arrived[1], gradient["rest"] = lax.optimization_barrier((arrived[1], gradient["rest"]))
        if chunk >= 1:
            arrived[chunk], mine[chunk - 1] = lax.optimization_barrier((arrived[chunk], mine[chunk - 1]))
        if chunk >= 2:
            arrived[chunk], far[chunk - 2], near[chunk - 2] = lax.optimization_barrier(
                (arrived[chunk], far[chunk - 2], near[chunk - 2])
            )
        if chunk < AHEAD:
            total = RATE * rows_of(gradient["first"], chunk)
        else:
            total = RATE * rows_of(gradient["rest"], chunk - AHEAD)
        for term in arrived[chunk]:
            total = total + term.astype(jnp.float32) / scale
        own = rows_of(weights, chunk) - total
        mine[chunk], sent = lax.optimization_barrier((own, (own * scale).astype(WIRE)))
        if chunk == 0:
            later, sent = lax.optimization_barrier((shard, sent))
            gradient["rest"] = partial(later, first, rows - first)
        after = chunk + AHEAD
        if after < CHUNKS:
            terms[after], sent = lax.optimization_barrier((terms[after], sent))
            arrived[after] = send_terms(terms[after])
        far[chunk] = swapped(sent, "blk", 1)
        near[chunk] = swapped(sent, "blk", 0)

    out = jnp.zeros_like(weights)
    for chunk in range(CHUNKS):
        mixed = (
            c_near * near[chunk].astype(jnp.float32)
            + c_self * mine[chunk]
            + c_far * far[chunk].astype(jnp.float32)
        )
        out = lax.dynamic_update_slice_in_dim(out, mixed, chunk * step, axis=0)
    return out[None]


def solution(mesh):
    return jax.shard_map(
        on_device,
        mesh=mesh,
        in_specs=(P("blk", "fsdp", None), P("blk", "fsdp", None), P("blk", "fsdp", None), P()),
        out_specs=P("blk", "fsdp", None),
        check_vma=False,
    )
```

```python
import math

import jax
import jax.numpy as jnp
from jax import lax
from jax.sharding import PartitionSpec as P

MIX_DENOM = 64
RATE = 0.03
LARGEST = 6.0
WIRE = jnp.float16
CHUNKS = 8
AHEAD = 2


def from_behind(value, axis, steps):
    count = lax.axis_size(axis)
    pairs = [(source, (source + steps) % count) for source in range(count)]
    return lax.ppermute(value, axis, pairs)


def swapped(value, axis, first):
    count = lax.axis_size(axis)
    pairs = []
    for source in range(first, count, 2):
        partner = (source + 1) % count
        pairs += [(source, partner), (partner, source)]
    return lax.ppermute(value, axis, pairs)


def wire_scale(tokens):
    bound = LARGEST + RATE * LARGEST * LARGEST * tokens
    return 2.0 ** math.floor(math.log2(float(jnp.finfo(WIRE).max) / bound))


def on_device(params, inputs, cotangent, mix):
    weights = params[0]
    features = inputs[0]
    cot_local = cotangent[0]
    rows = weights.shape[0]
    shards = lax.axis_size("fsdp")
    scale = wire_scale(features.shape[0] * shards)
    replica = lax.axis_index("blk")
    shard = lax.axis_index("fsdp")
    pick = (jnp.arange(lax.axis_size("blk")) == replica).astype(jnp.float32)
    coeff = jnp.dot(pick, mix.astype(jnp.float32), precision=lax.Precision.HIGHEST) / MIX_DENOM
    even = replica % 2 == 0
    c_self = coeff[1]
    c_near = jnp.where(even, coeff[2], coeff[0]) / scale
    c_far = jnp.where(even, coeff[0], coeff[2]) / scale
    step = rows // CHUNKS

    def partial(owner, first, count):
        block = lax.dynamic_slice_in_dim(features, owner * rows + first, count, axis=1)
        return lax.dot_general(
            block, cot_local, (((0,), (0,)), ((), ())), preferred_element_type=jnp.float32
        )

    def for_others(shard, first, count):
        return [
            (partial(lax.rem(shard + away, shards), first, count) * (RATE * scale)).astype(WIRE)
            for away in range(1, shards)
        ]

    def send_terms(terms):
        return [from_behind(term, "fsdp", away) for away, term in zip(range(1, shards), terms)]

    def rows_of(value, chunk):
        return value[chunk * step:(chunk + 1) * step]

    arrived = {}
    for chunk in range(AHEAD):
        arrived[chunk] = send_terms(for_others(shard, chunk * step, step))
    first = AHEAD * step
    gradient = {"first": partial(shard, 0, first)}
    rest = for_others(shard, first, rows - first)
    terms = {
        chunk: [rows_of(term, chunk - AHEAD) for term in rest] for chunk in range(AHEAD, CHUNKS)
    }
    mine = {}
    near = {}
    far = {}

    arrived[0], terms, gradient = lax.optimization_barrier((arrived[0], terms, gradient))
    for chunk in range(CHUNKS):
        if chunk == 1:
            arrived[1], gradient["rest"] = lax.optimization_barrier((arrived[1], gradient["rest"]))
        if chunk >= 1:
            arrived[chunk], mine[chunk - 1] = lax.optimization_barrier((arrived[chunk], mine[chunk - 1]))
        if chunk >= 2:
            arrived[chunk], far[chunk - 2], near[chunk - 2] = lax.optimization_barrier(
                (arrived[chunk], far[chunk - 2], near[chunk - 2])
            )
        if chunk < AHEAD:
            total = RATE * rows_of(gradient["first"], chunk)
        else:
            total = RATE * rows_of(gradient["rest"], chunk - AHEAD)
        for term in arrived[chunk]:
            total = total + term.astype(jnp.float32) / scale
        own = rows_of(weights, chunk) - total
        mine[chunk], sent = lax.optimization_barrier((own, (own * scale).astype(WIRE)))
        if chunk == 0:
            later, sent = lax.optimization_barrier((shard, sent))
            gradient["rest"] = partial(later, first, rows - first)
        after = chunk + AHEAD
        if after < CHUNKS:
            terms[after], sent = lax.optimization_barrier((terms[after], sent))
            arrived[after] = send_terms(terms[after])
        if chunk == CHUNKS - 1:
            far[0], near[0], sent = lax.optimization_barrier((far[0], near[0], sent))
        far[chunk] = swapped(sent, "blk", 1)
        near[chunk] = swapped(sent, "blk", 0)

    out = jnp.zeros_like(weights)
    for chunk in range(CHUNKS):
        mixed = (
            c_near * near[chunk].astype(jnp.float32)
            + c_self * mine[chunk]
            + c_far * far[chunk].astype(jnp.float32)
        )
        out = lax.dynamic_update_slice_in_dim(out, mixed, chunk * step, axis=0)
    return out[None]


def solution(mesh):
    return jax.shard_map(
        on_device,
        mesh=mesh,
        in_specs=(P("blk", "fsdp", None), P("blk", "fsdp", None), P("blk", "fsdp", None), P()),
        out_specs=P("blk", "fsdp", None),
        check_vma=False,
    )
```

```python
import functools
import math

import jax
import jax.numpy as jnp
from jax import lax
from jax.experimental import pallas as pl
from jax.experimental.pallas import tpu as pltpu
from jax.sharding import PartitionSpec as P

MIX_DENOM = 64
RATE = 0.03
LARGEST = 6.0
WIRE = jnp.float16
STEP = 256
TILE = 256
AHEAD = 2
EARLY = 3


def from_behind(value, axis, steps):
    count = lax.axis_size(axis)
    pairs = [(source, (source + steps) % count) for source in range(count)]
    return lax.ppermute(value, axis, pairs)


def swapped(value, axis, first):
    count = lax.axis_size(axis)
    pairs = []
    for source in range(first, count, 2):
        partner = (source + 1) % count
        pairs += [(source, partner), (partner, source)]
    return lax.ppermute(value, axis, pairs)


def wire_scale(tokens):
    bound = LARGEST + RATE * LARGEST * LARGEST * tokens
    return 2.0 ** math.floor(math.log2(float(jnp.finfo(WIRE).max) / bound))


def product_kernel(factor, offset_ref, features_ref, cot_ref, *rest):
    product = factor * lax.dot_general(
        features_ref[...], cot_ref[...], (((0,), (0,)), ((), ())), preferred_element_type=jnp.float32
    )
    out_ref = rest[-1]
    out_ref[...] = product if len(rest) == 1 else rest[0][...] + product


def product(features, cot, start, size, factor, added=None):
    tokens, width = cot.shape
    tile = math.gcd(size, TILE)
    by_rows = pl.BlockSpec((tile, width), lambda i, offset: (i, 0))
    specs = [
        pl.BlockSpec((tokens, tile), lambda i, offset: (0, offset[0] + i)),
        pl.BlockSpec((tokens, width), lambda i, offset: (0, 0)),
    ]
    operands = [features, cot]
    if added is not None:
        specs.append(by_rows)
        operands.append(added)
    return pl.pallas_call(
        functools.partial(product_kernel, factor),
        grid_spec=pltpu.PrefetchScalarGridSpec(
            num_scalar_prefetch=1, grid=(size // tile,), in_specs=specs, out_specs=by_rows
        ),
        out_shape=jax.ShapeDtypeStruct((size, width), jnp.float32),
        compiler_params=pltpu.CompilerParams(vmem_limit_bytes=24 * 2**20),
        cost_estimate=pl.CostEstimate(flops=0, bytes_accessed=0, transcendentals=0),
    )(jnp.reshape(start // tile, (1,)), *operands)


def on_device(params, inputs, cotangent, mix):
    weights = params[0]
    features = inputs[0]
    cot_local = cotangent[0]
    rows = weights.shape[0]
    shards = lax.axis_size("fsdp")
    scale = wire_scale(features.shape[0] * shards)
    replica = lax.axis_index("blk")
    shard = lax.axis_index("fsdp")
    pick = (jnp.arange(lax.axis_size("blk")) == replica).astype(jnp.float32)
    coeff = jnp.dot(pick, mix.astype(jnp.float32), precision=lax.Precision.HIGHEST) / MIX_DENOM
    even = replica % 2 == 0
    c_self = coeff[1]
    c_near = jnp.where(even, coeff[2], coeff[0]) / scale
    c_far = jnp.where(even, coeff[0], coeff[2]) / scale
    step = math.gcd(rows, STEP)
    chunks = rows // step
    early = min(EARLY, chunks)

    def rows_of(value, chunk):
        return value[chunk * step:(chunk + 1) * step]

    def for_others(shard, first, count):
        return [
            product(
                features, cot_local, lax.rem(shard + away, shards) * rows + first * step,
                count * step, RATE * scale,
            )
            for away in range(1, shards)
        ]

    def send_terms(made, place):
        return [
            from_behind(rows_of(term, place).astype(WIRE), "fsdp", away)
            for away, term in zip(range(1, shards), made)
        ]

    def u_of(chunk):
        total = rows_of(base, chunk)
        for term in arrived[chunk]:
            total = total - term.astype(jnp.float32) / scale
        return total

    def mix_into(out, chunk):
        mixed = (
            c_near * near[chunk].astype(jnp.float32)
            + c_self * u_of(chunk)
            + c_far * far[chunk].astype(jnp.float32)
        )
        return lax.dynamic_update_slice_in_dim(out, mixed, chunk * step, axis=0)

    near = {}
    far = {}
    made = for_others(shard, 0, early)
    arrived = {chunk: send_terms(made, chunk) for chunk in range(min(AHEAD, chunks))}
    made, later = lax.optimization_barrier((made, shard))
    base = product(features, cot_local, later * rows, rows, -RATE, weights)

    arrived[0], base = lax.optimization_barrier((arrived[0], base))
    for chunk in range(chunks):
        if chunk == 1 and early < chunks:
            arrived[1], rest = lax.optimization_barrier((arrived[1], rest))
        if chunk >= 2:
            arrived[chunk], far[chunk - 2], near[chunk - 2] = lax.optimization_barrier(
                (arrived[chunk], far[chunk - 2], near[chunk - 2])
            )
        sent = (u_of(chunk) * scale).astype(WIRE)
        sent, base, made, later = lax.optimization_barrier((sent, base, made, shard))
        if chunk == 0 and early < chunks:
            rest = for_others(later, early, chunks - early)
        after = chunk + AHEAD
        if after < early:
            arrived[after] = send_terms(made, after)
        elif after < chunks:
            rest, sent = lax.optimization_barrier((rest, sent))
            arrived[after] = send_terms(rest, after - early)
        if chunk == chunks - 1:
            far[0], near[0], sent = lax.optimization_barrier((far[0], near[0], sent))
        far[chunk] = swapped(sent, "blk", 1)
        near[chunk] = swapped(sent, "blk", 0)

    out = jnp.zeros_like(weights)
    for chunk in range(chunks):
        out = mix_into(out, chunk)
    return out[None]


def solution(mesh):
    return jax.shard_map(
        on_device,
        mesh=mesh,
        in_specs=(P("blk", "fsdp", None), P("blk", "fsdp", None), P("blk", "fsdp", None), P()),
        out_specs=P("blk", "fsdp", None),
        check_vma=False,
    )
```

```python
import functools
import math

import jax
import jax.numpy as jnp
from jax import lax
from jax.experimental import pallas as pl
from jax.experimental.pallas import tpu as pltpu
from jax.sharding import PartitionSpec as P

MIX_DENOM = 64
RATE = 0.03
LARGEST = 6.0
WIRE = jnp.float16
STEP = 256
TILE = 256
AHEAD = 2


def from_behind(value, axis, steps):
    count = lax.axis_size(axis)
    pairs = [(source, (source + steps) % count) for source in range(count)]
    return lax.ppermute(value, axis, pairs)


def swapped(value, axis, first):
    count = lax.axis_size(axis)
    pairs = []
    for source in range(first, count, 2):
        partner = (source + 1) % count
        pairs += [(source, partner), (partner, source)]
    return lax.ppermute(value, axis, pairs)


def wire_scale(tokens):
    bound = LARGEST + RATE * LARGEST * LARGEST * tokens
    return 2.0 ** math.floor(math.log2(float(jnp.finfo(WIRE).max) / bound))


def product_kernel(factor, offset_ref, features_ref, cot_ref, *rest):
    product = factor * lax.dot_general(
        features_ref[...], cot_ref[...], (((0,), (0,)), ((), ())), preferred_element_type=jnp.float32
    )
    out_ref = rest[-1]
    out_ref[...] = product if len(rest) == 1 else rest[0][...] + product


def product(features, cot, start, size, factor, added=None):
    tokens, width = cot.shape
    tile = math.gcd(size, TILE)
    by_rows = pl.BlockSpec((tile, width), lambda i, offset: (i, 0))
    specs = [
        pl.BlockSpec((tokens, tile), lambda i, offset: (0, offset[0] + i)),
        pl.BlockSpec((tokens, width), lambda i, offset: (0, 0)),
    ]
    operands = [features, cot]
    if added is not None:
        specs.append(by_rows)
        operands.append(added)
    return pl.pallas_call(
        functools.partial(product_kernel, factor),
        grid_spec=pltpu.PrefetchScalarGridSpec(
            num_scalar_prefetch=1, grid=(size // tile,), in_specs=specs, out_specs=by_rows
        ),
        out_shape=jax.ShapeDtypeStruct((size, width), jnp.float32),
        compiler_params=pltpu.CompilerParams(vmem_limit_bytes=56 * 2**20),
        cost_estimate=pl.CostEstimate(flops=0, bytes_accessed=0, transcendentals=0),
    )(jnp.reshape(start // tile, (1,)), *operands)


def on_device(params, inputs, cotangent, mix):
    weights = params[0]
    features = inputs[0]
    cot_local = cotangent[0]
    rows = weights.shape[0]
    shards = lax.axis_size("fsdp")
    scale = wire_scale(features.shape[0] * shards)
    replica = lax.axis_index("blk")
    shard = lax.axis_index("fsdp")
    pick = (jnp.arange(lax.axis_size("blk")) == replica).astype(jnp.float32)
    coeff = jnp.dot(pick, mix.astype(jnp.float32), precision=lax.Precision.HIGHEST) / MIX_DENOM
    even = replica % 2 == 0
    c_self = coeff[1]
    c_near = jnp.where(even, coeff[2], coeff[0]) / scale
    c_far = jnp.where(even, coeff[0], coeff[2]) / scale
    step = math.gcd(rows, STEP)
    chunks = rows // step
    early = min(AHEAD, chunks)

    def rows_of(value, chunk):
        return value[chunk * step:(chunk + 1) * step]

    def owner(shard, away):
        other = shard + away
        return jnp.where(other < shards, other, other - shards)

    def for_others(shard, first, count):
        made = count and [
            product(
                features, cot_local, owner(shard, away) * rows + first * step,
                count * step, RATE * scale,
            )
            for away in range(1, shards)
        ]
        return {
            first + place: [rows_of(term, place).astype(WIRE) for term in made]
            for place in range(count)
        }

    def send_terms(terms):
        return [from_behind(term, "fsdp", away) for away, term in zip(range(1, shards), terms)]

    def u_of(chunk):
        total = rows_of(base, chunk)
        for term in arrived[chunk]:
            total = total - term.astype(jnp.float32) / scale
        return total

    def mix_into(out, chunk):
        mixed = (
            c_near * near[chunk].astype(jnp.float32)
            + c_self * u_of(chunk)
            + c_far * far[chunk].astype(jnp.float32)
        )
        return lax.dynamic_update_slice_in_dim(out, mixed, chunk * step, axis=0)

    near = {}
    far = {}
    terms = for_others(shard, 0, early)
    arrived = {chunk: send_terms(terms[chunk]) for chunk in range(early)}
    terms, later = lax.optimization_barrier((terms, shard))
    base = product(features, cot_local, later * rows, rows, -RATE, weights)

    base, later = lax.optimization_barrier((base, shard))
    terms = for_others(later, early, chunks - early)
    arrived[0], base, terms = lax.optimization_barrier((arrived[0], base, terms))
    for chunk in range(chunks):
        if chunk >= 2:
            arrived[chunk], far[chunk - 2], near[chunk - 2] = lax.optimization_barrier(
                (arrived[chunk], far[chunk - 2], near[chunk - 2])
            )
        sent = (u_of(chunk) * scale).astype(WIRE)
        sent, base = lax.optimization_barrier((sent, base))
        after = chunk + early
        if after < chunks:
            terms[after], sent = lax.optimization_barrier((terms[after], sent))
            arrived[after] = send_terms(terms[after])
        if chunk == chunks - 1:
            far[0], near[0], sent = lax.optimization_barrier((far[0], near[0], sent))
        far[chunk] = swapped(sent, "blk", 1)
        near[chunk] = swapped(sent, "blk", 0)

    out = jnp.zeros_like(weights)
    for chunk in range(chunks):
        out = mix_into(out, chunk)
    return out[None]


def solution(mesh):
    return jax.shard_map(
        on_device,
        mesh=mesh,
        in_specs=(P("blk", "fsdp", None), P("blk", "fsdp", None), P("blk", "fsdp", None), P()),
        out_specs=P("blk", "fsdp", None),
        check_vma=False,
    )
```

```python
import math

import jax
import jax.numpy as jnp
from jax import lax
from jax.sharding import PartitionSpec as P

MIX_DENOM = 64
RATE = 0.03
LARGEST = 6.0
WIRE = jnp.float16
STEP = 256
AHEAD = 2


def from_behind(value, axis, steps):
    count = lax.axis_size(axis)
    pairs = [(source, (source + steps) % count) for source in range(count)]
    return lax.ppermute(value, axis, pairs)


def swapped(value, axis, first):
    count = lax.axis_size(axis)
    pairs = []
    for source in range(first, count, 2):
        partner = (source + 1) % count
        pairs += [(source, partner), (partner, source)]
    return lax.ppermute(value, axis, pairs)


def wire_scale(tokens):
    bound = LARGEST + RATE * LARGEST * LARGEST * tokens
    return 2.0 ** math.floor(math.log2(float(jnp.finfo(WIRE).max) / bound))


def on_device(params, inputs, cotangent, mix):
    weights = params[0]
    features = inputs[0]
    cot_local = cotangent[0]
    rows = weights.shape[0]
    shards = lax.axis_size("fsdp")
    scale = wire_scale(features.shape[0] * shards)
    replica = lax.axis_index("blk")
    shard = lax.axis_index("fsdp")
    pick = (jnp.arange(lax.axis_size("blk")) == replica).astype(jnp.float32)
    coeff = jnp.dot(pick, mix.astype(jnp.float32), precision=lax.Precision.HIGHEST) / MIX_DENOM
    even = replica % 2 == 0
    c_self = coeff[1]
    c_near = jnp.where(even, coeff[2], coeff[0]) / scale
    c_far = jnp.where(even, coeff[0], coeff[2]) / scale
    step = math.gcd(rows, STEP)
    chunks = rows // step

    def partial(owner, first, count):
        block = lax.dynamic_slice_in_dim(features, owner * rows + first, count, axis=1)
        return lax.dot_general(
            block, cot_local, (((0,), (0,)), ((), ())), preferred_element_type=jnp.float32
        )

    def owner(shard, away):
        other = shard + away
        return jnp.where(other < shards, other, other - shards)

    def for_others(shard, first, count):
        return [
            (partial(owner(shard, away), first, count) * (RATE * scale)).astype(WIRE)
            for away in range(1, shards)
        ]

    def send_terms(terms):
        return [from_behind(term, "fsdp", away) for away, term in zip(range(1, shards), terms)]

    def rows_of(value, chunk):
        return value[chunk * step:(chunk + 1) * step]

    def own_part(shard, first, count):
        return rows_from(weights, first, count) - RATE * partial(shard, first * step, count * step)

    def rows_from(value, first, count):
        return value[first * step:(first + count) * step]

    def u_of(chunk):
        total = rows_of(base[0], chunk) if chunk < split else rows_of(base[1], chunk - split)
        for term in arrived[chunk]:
            total = total - term.astype(jnp.float32) / scale
        return total

    split = min(2, chunks)
    early = min(AHEAD + 1, chunks)
    near = {}
    far = {}
    terms = {chunk: for_others(shard, chunk * step, step) for chunk in range(early)}
    arrived = {chunk: send_terms(terms[chunk]) for chunk in range(min(AHEAD, chunks))}
    base = [own_part(shard, 0, split)]

    arrived[0], base, terms = lax.optimization_barrier((arrived[0], base, terms))
    for chunk in range(chunks):
        if chunk in (1, 2):
            arrived[chunk], base, terms = lax.optimization_barrier((arrived[chunk], base, terms))
        if chunk == 1:
            arrived[1], far[0] = lax.optimization_barrier((arrived[1], far[0]))
        if chunk >= 2:
            arrived[chunk], far[chunk - 2], near[chunk - 2] = lax.optimization_barrier(
                (arrived[chunk], far[chunk - 2], near[chunk - 2])
            )
        sent = (u_of(chunk) * scale).astype(WIRE)
        sent, base, later = lax.optimization_barrier((sent, base, shard))
        if chunk == 0 and early < chunks:
            rest = for_others(later, early * step, rows - early * step)
            for after in range(early, chunks):
                terms[after] = [rows_of(term, after - early) for term in rest]
        if chunk == 1 and split < chunks:
            base.append(own_part(later, split, chunks - split))
        after = chunk + AHEAD
        if after < chunks:
            terms[after], sent = lax.optimization_barrier((terms[after], sent))
            arrived[after] = send_terms(terms[after])
        if chunk == chunks - 1:
            far[0], near[0], sent = lax.optimization_barrier((far[0], near[0], sent))
        far[chunk] = swapped(sent, "blk", 1)
        near[chunk] = swapped(sent, "blk", 0)

    out = jnp.zeros_like(weights)
    for chunk in range(chunks):
        mixed = (
            c_near * near[chunk].astype(jnp.float32)
            + c_self * u_of(chunk)
            + c_far * far[chunk].astype(jnp.float32)
        )
        out = lax.dynamic_update_slice_in_dim(out, mixed, chunk * step, axis=0)
    return out[None]


def solution(mesh):
    return jax.shard_map(
        on_device,
        mesh=mesh,
        in_specs=(P("blk", "fsdp", None), P("blk", "fsdp", None), P("blk", "fsdp", None), P()),
        out_specs=P("blk", "fsdp", None),
        check_vma=False,
    )
```

```python
import math

import jax
import jax.numpy as jnp
from jax import lax
from jax.sharding import PartitionSpec as P

MIX_DENOM = 64
RATE = 0.03
LARGEST = 6.0
WIRE = jnp.float16
STEP = 256
AHEAD = 2


def from_behind(value, axis, steps):
    count = lax.axis_size(axis)
    pairs = [(source, (source + steps) % count) for source in range(count)]
    return lax.ppermute(value, axis, pairs)


def swapped(value, axis, first):
    count = lax.axis_size(axis)
    pairs = []
    for source in range(first, count, 2):
        partner = (source + 1) % count
        pairs += [(source, partner), (partner, source)]
    return lax.ppermute(value, axis, pairs)


def wire_scale(tokens):
    bound = LARGEST + RATE * LARGEST * LARGEST * tokens
    return 2.0 ** math.floor(math.log2(float(jnp.finfo(WIRE).max) / bound))


def on_device(params, inputs, cotangent, mix):
    weights = params[0]
    features = inputs[0]
    cot_local = cotangent[0]
    rows = weights.shape[0]
    shards = lax.axis_size("fsdp")
    scale = wire_scale(features.shape[0] * shards)
    replica = lax.axis_index("blk")
    shard = lax.axis_index("fsdp")
    pick = (jnp.arange(lax.axis_size("blk")) == replica).astype(jnp.float32)
    coeff = jnp.dot(pick, mix.astype(jnp.float32), precision=lax.Precision.HIGHEST) / MIX_DENOM
    even = replica % 2 == 0
    c_self = coeff[1]
    c_near = jnp.where(even, coeff[2], coeff[0]) / scale
    c_far = jnp.where(even, coeff[0], coeff[2]) / scale
    step = math.gcd(rows, STEP)
    chunks = rows // step

    def partial(owner, first, count):
        block = lax.dynamic_slice_in_dim(features, owner * rows + first, count, axis=1)
        return lax.dot_general(
            block, cot_local, (((0,), (0,)), ((), ())), preferred_element_type=jnp.float32
        )

    def owner(shard, away):
        other = shard + away
        return jnp.where(other < shards, other, other - shards)

    def for_others(shard, first, count):
        return [
            (partial(owner(shard, away), first, count) * (RATE * scale)).astype(WIRE)
            for away in range(1, shards)
        ]

    def send_terms(terms):
        return [from_behind(term, "fsdp", away) for away, term in zip(range(1, shards), terms)]

    def rows_of(value, chunk):
        return value[chunk * step:(chunk + 1) * step]

    def own_part(shard, first, count):
        return rows_from(weights, first, count) - RATE * partial(shard, first * step, count * step)

    def rows_from(value, first, count):
        return value[first * step:(first + count) * step]

    def u_of(chunk):
        total = rows_of(base[0], chunk) if chunk < split else rows_of(base[1], chunk - split)
        for term in arrived[chunk]:
            total = total - term.astype(jnp.float32) / scale
        return total

    split = min(2, chunks)
    near = {}
    far = {}
    terms = {0: for_others(shard, 0, step)}
    arrived = {0: send_terms(terms[0])}
    rest = for_others(shard, step, rows - step) if chunks > 1 else []
    for chunk in range(1, chunks):
        terms[chunk] = [rows_of(term, chunk - 1) for term in rest]
    if chunks > 1:
        arrived[1] = send_terms(terms[1])
    base = [own_part(shard, 0, split)]

    arrived[0], base, terms = lax.optimization_barrier((arrived[0], base, terms))
    for chunk in range(chunks):
        if chunk == 1:
            arrived[1], base = lax.optimization_barrier((arrived[1], base))
        if chunk >= 2:
            arrived[chunk], far[chunk - 2], near[chunk - 2] = lax.optimization_barrier(
                (arrived[chunk], far[chunk - 2], near[chunk - 2])
            )
        sent = (u_of(chunk) * scale).astype(WIRE)
        sent, base, later = lax.optimization_barrier((sent, base, shard))
        if chunk == 0 and split < chunks:
            base.append(own_part(later, split, chunks - split))
        after = chunk + AHEAD
        if after < chunks:
            terms[after], sent = lax.optimization_barrier((terms[after], sent))
            arrived[after] = send_terms(terms[after])
        if chunk == chunks - 1:
            far[0], near[0], sent = lax.optimization_barrier((far[0], near[0], sent))
        far[chunk] = swapped(sent, "blk", 1)
        near[chunk] = swapped(sent, "blk", 0)

    out = jnp.zeros_like(weights)
    for chunk in range(chunks):
        mixed = (
            c_near * near[chunk].astype(jnp.float32)
            + c_self * u_of(chunk)
            + c_far * far[chunk].astype(jnp.float32)
        )
        out = lax.dynamic_update_slice_in_dim(out, mixed, chunk * step, axis=0)
    return out[None]


def solution(mesh):
    return jax.shard_map(
        on_device,
        mesh=mesh,
        in_specs=(P("blk", "fsdp", None), P("blk", "fsdp", None), P("blk", "fsdp", None), P()),
        out_specs=P("blk", "fsdp", None),
        check_vma=False,
    )
```

```python
import math

import jax
import jax.numpy as jnp
from jax import lax
from jax.sharding import PartitionSpec as P

MIX_DENOM = 64
RATE = 0.03
LARGEST = 6.0
WIRE = jnp.float16
STEP = 256
AHEAD = 3
LAG = 2
NLAG = 1


def from_behind(value, axis, steps):
    count = lax.axis_size(axis)
    pairs = [(source, (source + steps) % count) for source in range(count)]
    return lax.ppermute(value, axis, pairs)


def swapped(value, axis, first):
    count = lax.axis_size(axis)
    pairs = []
    for source in range(first, count, 2):
        partner = (source + 1) % count
        pairs += [(source, partner), (partner, source)]
    return lax.ppermute(value, axis, pairs)


def wire_scale(tokens):
    bound = LARGEST + RATE * LARGEST * LARGEST * tokens
    return 2.0 ** math.floor(math.log2(float(jnp.finfo(WIRE).max) / bound))


def on_device(params, inputs, cotangent, mix):
    weights = params[0]
    features = inputs[0]
    cot_local = cotangent[0]
    rows = weights.shape[0]
    shards = lax.axis_size("fsdp")
    scale = wire_scale(features.shape[0] * shards)
    replica = lax.axis_index("blk")
    shard = lax.axis_index("fsdp")
    pick = (jnp.arange(lax.axis_size("blk")) == replica).astype(jnp.float32)
    coeff = jnp.dot(pick, mix.astype(jnp.float32), precision=lax.Precision.HIGHEST) / MIX_DENOM
    even = replica % 2 == 0
    c_self = coeff[1]
    c_near = jnp.where(even, coeff[2], coeff[0]) / scale
    c_far = jnp.where(even, coeff[0], coeff[2]) / scale
    step = math.gcd(rows, STEP)
    chunks = rows // step

    def partial(owner, first, count):
        block = lax.dynamic_slice_in_dim(features, owner * rows + first, count, axis=1)
        return lax.dot_general(
            block, cot_local, (((0,), (0,)), ((), ())), preferred_element_type=jnp.float32
        )

    def owner(shard, away):
        other = shard + away
        return jnp.where(other < shards, other, other - shards)

    def for_others(shard, first, count):
        return [
            (partial(owner(shard, away), first, count) * (RATE * scale)).astype(WIRE)
            for away in range(1, shards)
        ]

    def send_terms(terms):
        return [from_behind(term, "fsdp", away) for away, term in zip(range(1, shards), terms)]

    def rows_of(value, chunk):
        return value[chunk * step:(chunk + 1) * step]

    def own_part(shard, first, count):
        return rows_from(weights, first, count) - RATE * partial(shard, first * step, count * step)

    def rows_from(value, first, count):
        return value[first * step:(first + count) * step]

    def u_of(chunk):
        total = rows_of(base[0], chunk) if chunk < split else rows_of(base[1], chunk - split)
        for term in arrived[chunk]:
            total = total - term.astype(jnp.float32) / scale
        return total

    split = min(2, chunks)
    near = {}
    far = {}
    terms = {0: for_others(shard, 0, step)}
    arrived = {0: send_terms(terms[0])}
    rest = for_others(shard, step, rows - step) if chunks > 1 else []
    for chunk in range(1, chunks):
        terms[chunk] = [rows_of(term, chunk - 1) for term in rest]
    for chunk in range(1, min(AHEAD, chunks)):
        arrived[chunk] = send_terms(terms[chunk])
    base = [own_part(shard, 0, split)]

    arrived[0], base, terms = lax.optimization_barrier((arrived[0], base, terms))
    for chunk in range(chunks):
        if chunk == 1:
            arrived[1], base = lax.optimization_barrier((arrived[1], base))
        if chunk >= LAG:
            arrived[chunk], far[chunk - LAG] = lax.optimization_barrier((arrived[chunk], far[chunk - LAG]))
        if chunk >= NLAG:
            arrived[chunk], near[chunk - NLAG] = lax.optimization_barrier((arrived[chunk], near[chunk - NLAG]))
        sent = (u_of(chunk) * scale).astype(WIRE)
        sent, base, later = lax.optimization_barrier((sent, base, shard))
        if chunk == 0 and split < chunks:
            base.append(own_part(later, split, chunks - split))
        after = chunk + AHEAD
        if after < chunks:
            terms[after], sent = lax.optimization_barrier((terms[after], sent))
            arrived[after] = send_terms(terms[after])
        if chunk == chunks - 1:
            far[0], near[0], sent = lax.optimization_barrier((far[0], near[0], sent))
        far[chunk] = swapped(sent, "blk", 1)
        near[chunk] = swapped(sent, "blk", 0)

    out = jnp.zeros_like(weights)
    for chunk in range(chunks):
        mixed = (
            c_near * near[chunk].astype(jnp.float32)
            + c_self * u_of(chunk)
            + c_far * far[chunk].astype(jnp.float32)
        )
        out = lax.dynamic_update_slice_in_dim(out, mixed, chunk * step, axis=0)
    return out[None]


def solution(mesh):
    return jax.shard_map(
        on_device,
        mesh=mesh,
        in_specs=(P("blk", "fsdp", None), P("blk", "fsdp", None), P("blk", "fsdp", None), P()),
        out_specs=P("blk", "fsdp", None),
        check_vma=False,
    )
```

```python
import math

import jax
import jax.numpy as jnp
from jax import lax
from jax.sharding import PartitionSpec as P

MIX_DENOM = 64
RATE = 0.03
LARGEST = 6.0
WIRE = jnp.float16
STEP = 256
AHEAD = 3
LAG = 2
NLAG = 1
MIXLAG = 3
EARLY = 1


def from_behind(value, axis, steps):
    count = lax.axis_size(axis)
    pairs = [(source, (source + steps) % count) for source in range(count)]
    return lax.ppermute(value, axis, pairs)


def swapped(value, axis, first):
    count = lax.axis_size(axis)
    pairs = []
    for source in range(first, count, 2):
        partner = (source + 1) % count
        pairs += [(source, partner), (partner, source)]
    return lax.ppermute(value, axis, pairs)


def wire_scale(tokens):
    bound = LARGEST + RATE * LARGEST * LARGEST * tokens
    return 2.0 ** math.floor(math.log2(float(jnp.finfo(WIRE).max) / bound))


def on_device(params, inputs, cotangent, mix):
    weights = params[0]
    features = inputs[0]
    cot_local = cotangent[0]
    rows = weights.shape[0]
    shards = lax.axis_size("fsdp")
    scale = wire_scale(features.shape[0] * shards)
    replica = lax.axis_index("blk")
    shard = lax.axis_index("fsdp")
    pick = (jnp.arange(lax.axis_size("blk")) == replica).astype(jnp.float32)
    coeff = jnp.dot(pick, mix.astype(jnp.float32), precision=lax.Precision.HIGHEST) / MIX_DENOM
    even = replica % 2 == 0
    c_self = coeff[1]
    c_near = jnp.where(even, coeff[2], coeff[0]) / scale
    c_far = jnp.where(even, coeff[0], coeff[2]) / scale
    step = math.gcd(rows, STEP)
    chunks = rows // step

    def partial(owner, first, count):
        block = lax.dynamic_slice_in_dim(features, owner * rows + first, count, axis=1)
        return lax.dot_general(
            block, cot_local, (((0,), (0,)), ((), ())), preferred_element_type=jnp.float32
        )

    def owner(shard, away):
        other = shard + away
        return jnp.where(other < shards, other, other - shards)

    def for_others(shard, first, count):
        return [
            (partial(owner(shard, away), first, count) * (RATE * scale)).astype(WIRE)
            for away in range(1, shards)
        ]

    def send_terms(terms):
        return [from_behind(term, "fsdp", away) for away, term in zip(range(1, shards), terms)]

    def rows_of(value, chunk):
        return value[chunk * step:(chunk + 1) * step]

    def own_part(shard, first, count):
        return rows_from(weights, first, count) - RATE * partial(shard, first * step, count * step)

    def rows_from(value, first, count):
        return value[first * step:(first + count) * step]

    def u_of(chunk):
        total = rows_of(base[0], chunk) if chunk < split else rows_of(base[1], chunk - split)
        for term in arrived[chunk]:
            total = total - term.astype(jnp.float32) / scale
        return total

    split = min(2, chunks)
    near = {}
    far = {}
    out = jnp.zeros_like(weights)
    mixed = 0

    def mix_into(out, chunk):
        value = (
            c_near * near[chunk].astype(jnp.float32)
            + c_self * u_of(chunk)
            + c_far * far[chunk].astype(jnp.float32)
        )
        return lax.dynamic_update_slice_in_dim(out, value, chunk * step, axis=0)

    early = min(EARLY, chunks)
    terms = {chunk: for_others(shard, chunk * step, step) for chunk in range(early)}
    arrived = {chunk: send_terms(terms[chunk]) for chunk in range(min(AHEAD, early))}
    if early < chunks:
        rest = for_others(shard, early * step, rows - early * step)
        for after in range(early, chunks):
            terms[after] = [rows_of(term, after - early) for term in rest]
        for after in range(early, min(AHEAD, chunks)):
            arrived[after] = send_terms(terms[after])
    base = [own_part(shard, 0, split)]

    arrived[0], base, terms = lax.optimization_barrier((arrived[0], base, terms))
    for chunk in range(chunks):
        if chunk == 1:
            arrived[1], base = lax.optimization_barrier((arrived[1], base))
        if chunk >= LAG:
            arrived[chunk], far[chunk - LAG] = lax.optimization_barrier((arrived[chunk], far[chunk - LAG]))
        if chunk >= NLAG:
            arrived[chunk], near[chunk - NLAG] = lax.optimization_barrier((arrived[chunk], near[chunk - NLAG]))
        if mixed:
            arrived[chunk], out = lax.optimization_barrier((arrived[chunk], out))
        sent = (u_of(chunk) * scale).astype(WIRE)
        sent, base, out, later = lax.optimization_barrier((sent, base, out, shard))
        if chunk == 0 and split < chunks:
            base.append(own_part(later, split, chunks - split))
        after = chunk + AHEAD
        if after < chunks:
            terms[after], sent = lax.optimization_barrier((terms[after], sent))
            arrived[after] = send_terms(terms[after])
        far[chunk] = swapped(sent, "blk", 1)
        near[chunk] = swapped(sent, "blk", 0)
        if chunk >= MIXLAG:
            out = mix_into(out, mixed)
            mixed += 1

    for chunk in range(mixed, chunks):
        out = mix_into(out, chunk)
    return out[None]


def solution(mesh):
    return jax.shard_map(
        on_device,
        mesh=mesh,
        in_specs=(P("blk", "fsdp", None), P("blk", "fsdp", None), P("blk", "fsdp", None), P()),
        out_specs=P("blk", "fsdp", None),
        check_vma=False,
    )
```

```python
import math

import jax
import jax.numpy as jnp
from jax import lax
from jax.sharding import PartitionSpec as P

MIX_DENOM = 64
RATE = 0.03
LARGEST = 6.0
WIRE = jnp.float16
STEP = 256
FIRST = 256
AHEAD = 3
MIXLAG = 5


def from_behind(value, axis, steps):
    count = lax.axis_size(axis)
    pairs = [(source, (source + steps) % count) for source in range(count)]
    return lax.ppermute(value, axis, pairs)


def swapped(value, axis, first):
    count = lax.axis_size(axis)
    pairs = []
    for source in range(first, count, 2):
        partner = (source + 1) % count
        pairs += [(source, partner), (partner, source)]
    return lax.ppermute(value, axis, pairs)


def wire_scale(tokens):
    bound = LARGEST + RATE * LARGEST * LARGEST * tokens
    return 2.0 ** math.floor(math.log2(float(jnp.finfo(WIRE).max) / bound))


def on_device(params, inputs, cotangent, mix):
    weights = params[0]
    features = inputs[0]
    cot_local = cotangent[0]
    rows = weights.shape[0]
    shards = lax.axis_size("fsdp")
    scale = wire_scale(features.shape[0] * shards)
    replica = lax.axis_index("blk")
    shard = lax.axis_index("fsdp")
    row = lax.dynamic_slice_in_dim(mix, replica, 1, axis=0).astype(jnp.float32) / MIX_DENOM
    left, own, right = row[:, 0:1], row[:, 1:2], row[:, 2:3]
    even = replica % 2 == 0
    sides = [jnp.where(even, right, left) / scale, own, jnp.where(even, left, right) / scale]
    coeff = jnp.broadcast_to(jnp.concatenate(sides, axis=0), (3, weights.shape[1]))
    first = min(FIRST, rows // 2)
    main = rows - first
    cuts = list(range(0, main, STEP)) + [main]
    chunks = len(cuts) - 1

    def owner(away, shard=shard):
        other = shard + away
        return jnp.where(other < shards, other, other - shards)

    def partial(owner, start, size):
        block = lax.dynamic_slice_in_dim(features, owner * rows + start, size, axis=1)
        return lax.dot_general(
            block, cot_local, (((0,), (0,)), ((), ())), preferred_element_type=jnp.float32
        )

    def for_others(start, stop):
        return [
            (partial(owner(away), start, stop - start) * (RATE * scale)).astype(WIRE)
            for away in range(1, shards)
        ]

    def own_part(shard, start, stop):
        return weights[start:stop] - RATE * partial(shard, start, stop - start)

    def add_over_fsdp(terms):
        return [from_behind(term, "fsdp", away) for away, term in zip(range(1, shards), terms)]

    def u_of(chunk):
        start, stop = cuts[chunk], cuts[chunk + 1]
        total = base[0][start:stop] if stop <= split else base[1][start - split:stop - split]
        for term in arrived[chunk]:
            total = total - term.astype(jnp.float32) / scale
        return total

    def mixture(near, own, far):
        return (
            coeff[0:1] * near.astype(jnp.float32) + coeff[1:2] * own + coeff[2:3] * far.astype(jnp.float32)
        )

    def mix_into(out, chunk):
        value = mixture(near[chunk], u_of(chunk), far[chunk])
        return lax.dynamic_update_slice_in_dim(out, value, cuts[chunk], axis=0)

    near = {}
    far = {}
    mixed = 0
    out = jnp.zeros_like(weights)
    split = cuts[min(2, chunks)]
    terms = {0: for_others(0, cuts[1])}
    arrived = {0: add_over_fsdp(terms[0])}

    parts = [own_part(shard, main, rows)]
    parts += [-RATE * partial(owner(away), main, first) for away in range(1, shards)]
    parts = jnp.concatenate(parts, axis=0)
    parts, sent = lax.optimization_barrier((parts, (parts * scale).astype(WIRE)))
    far[-1] = swapped(sent, "blk", 1)
    near[-1] = swapped(sent, "blk", 0)

    if chunks > 1:
        parts, later = lax.optimization_barrier((parts, shard))
        rest = [
            (partial(owner(away, later), cuts[1], main - cuts[1]) * (RATE * scale)).astype(WIRE)
            for away in range(1, shards)
        ]
        for chunk in range(1, chunks):
            terms[chunk] = [term[cuts[chunk] - cuts[1]:cuts[chunk + 1] - cuts[1]] for term in rest]
        for chunk in range(1, min(AHEAD, chunks)):
            if chunk == 2:
                terms[chunk], near[-1] = lax.optimization_barrier((terms[chunk], near[-1]))
            arrived[chunk] = add_over_fsdp(terms[chunk])
    base = [own_part(shard, 0, split)]

    arrived[0], base, terms = lax.optimization_barrier((arrived[0], base, terms))
    for chunk in range(chunks):
        if chunk == 1:
            arrived[1], base = lax.optimization_barrier((arrived[1], base))
        if chunk >= 1:
            arrived[chunk], far[chunk - 2] = lax.optimization_barrier((arrived[chunk], far[chunk - 2]))
        arrived[chunk], near[chunk - 1] = lax.optimization_barrier((arrived[chunk], near[chunk - 1]))
        if mixed:
            arrived[chunk], out = lax.optimization_barrier((arrived[chunk], out))
        if chunk == 3:
            arrived[chunk], parts = lax.optimization_barrier((arrived[chunk], parts))
        sent = (u_of(chunk) * scale).astype(WIRE)
        sent, base, out, later = lax.optimization_barrier((sent, base, out, shard))
        if chunk == 0 and split < main:
            base.append(own_part(later, split, main))
        if chunk == min(1, chunks - 1):
            coeff, parts, sent = lax.optimization_barrier((coeff, parts, sent))
            parts = mixture(near[-1], parts, far[-1])
            back = [
                (parts[away * first:(away + 1) * first] * scale).astype(WIRE) for away in range(1, shards)
            ]
            parts = parts[:first]
        after = chunk + AHEAD
        if after < chunks:
            terms[after], sent = lax.optimization_barrier((terms[after], sent))
            arrived[after] = add_over_fsdp(terms[after])
        if after == max(chunks, AHEAD):
            back, sent = lax.optimization_barrier((back, sent))
            back = add_over_fsdp(back)
        far[chunk] = swapped(sent, "blk", 1)
        near[chunk] = swapped(sent, "blk", 0)
        if chunk >= MIXLAG:
            out = mix_into(out, mixed)
            mixed += 1

    for term in back:
        parts = parts + term.astype(jnp.float32) / scale
    out = lax.dynamic_update_slice_in_dim(out, parts, main, axis=0)
    for chunk in range(mixed, chunks):
        out = mix_into(out, chunk)
    return out[None]


def solution(mesh):
    return jax.shard_map(
        on_device,
        mesh=mesh,
        in_specs=(P("blk", "fsdp", None), P("blk", "fsdp", None), P("blk", "fsdp", None), P()),
        out_specs=P("blk", "fsdp", None),
        check_vma=False,
    )
```

```python
import math

import jax
import jax.numpy as jnp
from jax import lax
from jax.sharding import PartitionSpec as P

MIX_DENOM = 64
RATE = 0.03
LARGEST = 6.0
WIRE = jnp.float16
STEP = 240
FIRST = 192
AHEAD = 3
MIXLAG = 5


def from_behind(value, axis, steps):
    count = lax.axis_size(axis)
    pairs = [(source, (source + steps) % count) for source in range(count)]
    return lax.ppermute(value, axis, pairs)


def swapped(value, axis, first):
    count = lax.axis_size(axis)
    pairs = []
    for source in range(first, count, 2):
        partner = (source + 1) % count
        pairs += [(source, partner), (partner, source)]
    return lax.ppermute(value, axis, pairs)


def wire_scale(tokens):
    bound = LARGEST + RATE * LARGEST * LARGEST * tokens
    return 2.0 ** math.floor(math.log2(float(jnp.finfo(WIRE).max) / bound))


def on_device(params, inputs, cotangent, mix):
    weights = params[0]
    features = inputs[0]
    cot_local = cotangent[0]
    rows = weights.shape[0]
    shards = lax.axis_size("fsdp")
    scale = wire_scale(features.shape[0] * shards)
    replica = lax.axis_index("blk")
    shard = lax.axis_index("fsdp")
    def coefficients(mix):
        row = lax.dynamic_slice_in_dim(mix, replica, 1, axis=0).astype(jnp.float32) / MIX_DENOM
        left, own, right = row[:, 0:1], row[:, 1:2], row[:, 2:3]
        even = replica % 2 == 0
        sides = [jnp.where(even, right, left) / scale, own, jnp.where(even, left, right) / scale]
        return jnp.broadcast_to(jnp.concatenate(sides, axis=0), (3, weights.shape[1]))

    first = min(FIRST, rows // 2)
    main = rows - first
    cuts = list(range(0, main, STEP)) + [main]
    chunks = len(cuts) - 1
    middle = min(1, chunks - 1)

    def owner(away, shard=shard):
        other = shard + away
        return jnp.where(other < shards, other, other - shards)

    def partial(owner, start, size):
        block = lax.dynamic_slice_in_dim(features, owner * rows + start, size, axis=1)
        return lax.dot_general(
            block, cot_local, (((0,), (0,)), ((), ())), preferred_element_type=jnp.float32
        )

    def for_others(start, stop):
        return [
            (partial(owner(away), start, stop - start) * (RATE * scale)).astype(WIRE)
            for away in range(1, shards)
        ]

    def own_part(shard, start, stop):
        return weights[start:stop] - RATE * partial(shard, start, stop - start)

    def add_over_fsdp(terms):
        return [from_behind(term, "fsdp", away) for away, term in zip(range(1, shards), terms)]

    def u_of(chunk):
        start, stop = cuts[chunk], cuts[chunk + 1]
        total = base[0][start:stop] if stop <= split else base[1][start - split:stop - split]
        for term in arrived[chunk]:
            total = total - term.astype(jnp.float32) / scale
        return total

    def mixture(near, own, far):
        return (
            coeff[0:1] * near.astype(jnp.float32) + coeff[1:2] * own + coeff[2:3] * far.astype(jnp.float32)
        )

    def mix_into(out, chunk):
        value = mixture(near[chunk], u_of(chunk), far[chunk])
        return lax.dynamic_update_slice_in_dim(out, value, cuts[chunk], axis=0)

    near = {}
    far = {}
    mixed = 0
    out = jnp.zeros_like(weights)
    split = cuts[min(2, chunks)]
    terms = {0: for_others(0, cuts[1])}

    terms[0], later = lax.optimization_barrier((terms[0], shard))
    arrived = {0: add_over_fsdp(terms[0])}
    parts = [own_part(later, main, rows)]
    parts += [-RATE * partial(owner(away, later), main, first) for away in range(1, shards)]
    parts = jnp.concatenate(parts, axis=0)
    parts, sent = lax.optimization_barrier((parts, (parts * scale).astype(WIRE)))
    far[-1] = swapped(sent, "blk", 1)
    near[-1] = swapped(sent, "blk", 0)

    if chunks > 1:
        parts, later = lax.optimization_barrier((parts, shard))
        rest = [
            (partial(owner(away, later), cuts[1], main - cuts[1]) * (RATE * scale)).astype(WIRE)
            for away in range(1, shards)
        ]
        for chunk in range(1, chunks):
            terms[chunk] = [term[cuts[chunk] - cuts[1]:cuts[chunk + 1] - cuts[1]] for term in rest]
        for chunk in range(1, min(AHEAD, chunks)):
            if chunk == 2:
                terms[chunk], near[-1] = lax.optimization_barrier((terms[chunk], near[-1]))
            arrived[chunk] = add_over_fsdp(terms[chunk])
    base = [own_part(shard, 0, split)]

    arrived[0], base, terms = lax.optimization_barrier((arrived[0], base, terms))
    for chunk in range(chunks):
        if chunk == 1:
            arrived[1], base = lax.optimization_barrier((arrived[1], base))
        if chunk >= 1:
            arrived[chunk], far[chunk - 2] = lax.optimization_barrier((arrived[chunk], far[chunk - 2]))
        arrived[chunk], near[chunk - 1] = lax.optimization_barrier((arrived[chunk], near[chunk - 1]))
        if mixed:
            arrived[chunk], out = lax.optimization_barrier((arrived[chunk], out))
        if chunk == 3:
            arrived[chunk], parts = lax.optimization_barrier((arrived[chunk], parts))
        sent = (u_of(chunk) * scale).astype(WIRE)
        sent, base, out, later = lax.optimization_barrier((sent, base, out, shard))
        if chunk == 0 and split < main:
            base.append(own_part(later, split, main))
        if chunk == middle:
            mix, parts, sent = lax.optimization_barrier((mix, parts, sent))
            coeff = lax.optimization_barrier(coefficients(mix))
            parts = mixture(near[-1], parts, far[-1])
            back = [
                (parts[away * first:(away + 1) * first] * scale).astype(WIRE) for away in range(1, shards)
            ]
            parts = parts[:first]
        after = chunk + AHEAD
        if after < chunks:
            terms[after], sent = lax.optimization_barrier((terms[after], sent))
            arrived[after] = add_over_fsdp(terms[after])
        if chunk == max(chunks - AHEAD, middle):
            back, sent = lax.optimization_barrier((back, sent))
            back = add_over_fsdp(back)
        far[chunk] = swapped(sent, "blk", 1)
        near[chunk] = swapped(sent, "blk", 0)
        if chunk >= MIXLAG:
            out = mix_into(out, mixed)
            mixed += 1

    for term in back:
        parts = parts + term.astype(jnp.float32) / scale
    out = lax.dynamic_update_slice_in_dim(out, parts, main, axis=0)
    for chunk in range(mixed, chunks):
        out = mix_into(out, chunk)
    return out[None]


def solution(mesh):
    return jax.shard_map(
        on_device,
        mesh=mesh,
        in_specs=(P("blk", "fsdp", None), P("blk", "fsdp", None), P("blk", "fsdp", None), P()),
        out_specs=P("blk", "fsdp", None),
        check_vma=False,
    )
```

```python
import math

import jax
import jax.numpy as jnp
from jax import lax
from jax.sharding import PartitionSpec as P

MIX_DENOM = 64
RATE = 0.03
LARGEST = 6.0
WIRE = jnp.float16
STEP = 256
FIRST = 128
AHEAD = 3
MIXLAG = 99


def from_behind(value, axis, steps):
    count = lax.axis_size(axis)
    pairs = [(source, (source + steps) % count) for source in range(count)]
    return lax.ppermute(value, axis, pairs)


def swapped(value, axis, first):
    count = lax.axis_size(axis)
    pairs = []
    for source in range(first, count, 2):
        partner = (source + 1) % count
        pairs += [(source, partner), (partner, source)]
    return lax.ppermute(value, axis, pairs)


def wire_scale(tokens):
    bound = LARGEST + RATE * LARGEST * LARGEST * tokens
    return 2.0 ** math.floor(math.log2(float(jnp.finfo(WIRE).max) / bound))


def on_device(params, inputs, cotangent, mix):
    weights = params[0]
    features = inputs[0]
    cot_local = cotangent[0]
    rows = weights.shape[0]
    shards = lax.axis_size("fsdp")
    scale = wire_scale(features.shape[0] * shards)
    replica = lax.axis_index("blk")
    shard = lax.axis_index("fsdp")
    def coefficients(mix):
        row = lax.dynamic_slice_in_dim(mix, replica, 1, axis=0).astype(jnp.float32)
        row = jnp.where(replica % 2 == 0, row[:, ::-1], row)
        column = jnp.reshape(row, (3, 1)) / MIX_DENOM
        return jnp.broadcast_to(column, (3, weights.shape[1]))

    first = min(FIRST, rows // 2)
    main = rows - first
    cuts = list(range(0, main, STEP)) + [main]
    chunks = len(cuts) - 1
    middle = min(1, chunks - 1)

    def owner(away, shard=shard):
        other = shard + away
        return jnp.where(other < shards, other, other - shards)

    def partial(owner, start, size):
        block = lax.dynamic_slice_in_dim(features, owner * rows + start, size, axis=1)
        return lax.dot_general(
            block, cot_local, (((0,), (0,)), ((), ())), preferred_element_type=jnp.float32
        )

    def for_others(start, stop):
        return [
            (partial(owner(away), start, stop - start) * (RATE * scale)).astype(WIRE)
            for away in range(1, shards)
        ]

    def own_part(shard, start, stop):
        return weights[start:stop] - RATE * partial(shard, start, stop - start)

    def add_over_fsdp(terms):
        return [from_behind(term, "fsdp", away) for away, term in zip(range(1, shards), terms)]

    def u_of(chunk):
        start, stop = cuts[chunk], cuts[chunk + 1]
        total = base[0][start:stop] if stop <= split else base[1][start - split:stop - split]
        for term in arrived[chunk]:
            total = total - term.astype(jnp.float32) / scale
        return total

    def mixture(near, own, far):
        return (
            coeff[0:1] * (near.astype(jnp.float32) / scale)
            + coeff[1:2] * own
            + coeff[2:3] * (far.astype(jnp.float32) / scale)
        )

    def mix_into(out, chunk):
        value = mixture(near[chunk], u_of(chunk), far[chunk])
        return lax.dynamic_update_slice_in_dim(out, value, cuts[chunk], axis=0)

    near = {}
    far = {}
    mixed = 0
    out = jnp.zeros_like(weights)
    split = cuts[min(2, chunks)]
    terms = {0: for_others(0, cuts[1])}

    terms[0], later = lax.optimization_barrier((terms[0], shard))
    arrived = {0: add_over_fsdp(terms[0])}
    parts = [own_part(later, main, rows)]
    parts += [-RATE * partial(owner(away, later), main, first) for away in range(1, shards)]
    parts = jnp.concatenate(parts, axis=0)
    parts, sent = lax.optimization_barrier((parts, (parts * scale).astype(WIRE)))
    far[-1] = swapped(sent, "blk", 1)
    near[-1] = swapped(sent, "blk", 0)

    if chunks > 1:
        parts, later = lax.optimization_barrier((parts, shard))
        rest = [
            (partial(owner(away, later), cuts[1], rows - cuts[1]) * (RATE * scale)).astype(WIRE)
            for away in range(1, shards)
        ]
        for chunk in range(1, chunks):
            terms[chunk] = [term[cuts[chunk] - cuts[1]:cuts[chunk + 1] - cuts[1]] for term in rest]
        for chunk in range(1, min(AHEAD, chunks)):
            if chunk == 2:
                terms[chunk], near[-1] = lax.optimization_barrier((terms[chunk], near[-1]))
            arrived[chunk] = add_over_fsdp(terms[chunk])
    base = [own_part(shard, 0, split)]

    arrived[0], base, terms = lax.optimization_barrier((arrived[0], base, terms))
    for chunk in range(chunks):
        if chunk == 1:
            arrived[1], base = lax.optimization_barrier((arrived[1], base))
        if chunk >= 1:
            arrived[chunk], far[chunk - 2] = lax.optimization_barrier((arrived[chunk], far[chunk - 2]))
        arrived[chunk], near[chunk - 1] = lax.optimization_barrier((arrived[chunk], near[chunk - 1]))
        if mixed:
            arrived[chunk], out = lax.optimization_barrier((arrived[chunk], out))
        if chunk == 3:
            arrived[chunk], parts = lax.optimization_barrier((arrived[chunk], parts))
        sent = (u_of(chunk) * scale).astype(WIRE)
        sent, base, out, later = lax.optimization_barrier((sent, base, out, shard))
        if chunk == 0 and split < main:
            base.append(own_part(later, split, rows))
        if chunk == middle:
            mix, parts, sent = lax.optimization_barrier((mix, parts, sent))
            coeff = lax.optimization_barrier(coefficients(mix))
            parts = mixture(near[-1], parts, far[-1])
            back = [
                (parts[away * first:(away + 1) * first] * scale).astype(WIRE) for away in range(1, shards)
            ]
            parts = parts[:first]
        after = chunk + AHEAD
        if after < chunks:
            terms[after], sent = lax.optimization_barrier((terms[after], sent))
            arrived[after] = add_over_fsdp(terms[after])
        if chunk == max(chunks - AHEAD, middle):
            back, sent = lax.optimization_barrier((back, sent))
            back = add_over_fsdp(back)
        far[chunk] = swapped(sent, "blk", 1)
        near[chunk] = swapped(sent, "blk", 0)
        if chunk >= MIXLAG:
            out = mix_into(out, mixed)
            mixed += 1

    for term in back:
        parts = parts + term.astype(jnp.float32) / scale
    out = lax.dynamic_update_slice_in_dim(out, parts, main, axis=0)
    for chunk in range(mixed, chunks):
        out = mix_into(out, chunk)
    return out[None]


def solution(mesh):
    return jax.shard_map(
        on_device,
        mesh=mesh,
        in_specs=(P("blk", "fsdp", None), P("blk", "fsdp", None), P("blk", "fsdp", None), P()),
        out_specs=P("blk", "fsdp", None),
        check_vma=False,
    )
```

```python
import math

import jax
import jax.numpy as jnp
from jax import lax
from jax.sharding import PartitionSpec as P

MIX_DENOM = 64
RATE = 0.03
LARGEST = 6.0
WIRE = jnp.float16
STEP = 256
FIRST = 256
AHEAD = 3
MIXLAG = 99


def from_behind(value, axis, steps):
    count = lax.axis_size(axis)
    pairs = [(source, (source + steps) % count) for source in range(count)]
    return lax.ppermute(value, axis, pairs)


def swapped(value, axis, first):
    count = lax.axis_size(axis)
    pairs = []
    for source in range(first, count, 2):
        partner = (source + 1) % count
        pairs += [(source, partner), (partner, source)]
    return lax.ppermute(value, axis, pairs)


def wire_scale(tokens):
    bound = LARGEST + RATE * LARGEST * LARGEST * tokens
    return 2.0 ** math.floor(math.log2(float(jnp.finfo(WIRE).max) / bound))


def on_device(params, inputs, cotangent, mix):
    weights = params[0]
    features = inputs[0]
    cot_local = cotangent[0]
    rows = weights.shape[0]
    shards = lax.axis_size("fsdp")
    scale = wire_scale(features.shape[0] * shards)
    replica = lax.axis_index("blk")
    shard = lax.axis_index("fsdp")
    def coefficients(mix):
        row = lax.dynamic_slice_in_dim(mix, replica, 1, axis=0).astype(jnp.float32)
        row = jnp.where(replica % 2 == 0, row[:, ::-1], row)
        column = jnp.reshape(row, (3, 1)) / MIX_DENOM
        return jnp.broadcast_to(column, (3, weights.shape[1]))

    first = min(FIRST, rows // 2)
    main = rows - first
    cuts = list(range(0, main, STEP)) + [main]
    chunks = len(cuts) - 1
    middle = min(1, chunks - 1)

    def owner(away, shard=shard):
        other = shard + away
        return jnp.where(other < shards, other, other - shards)

    def partial(owner, start, size):
        block = lax.dynamic_slice_in_dim(features, owner * rows + start, size, axis=1)
        return lax.dot_general(
            block, cot_local, (((0,), (0,)), ((), ())), preferred_element_type=jnp.float32
        )

    def for_others(start, stop):
        return [
            (partial(owner(away), start, stop - start) * (RATE * scale)).astype(WIRE)
            for away in range(1, shards)
        ]

    def own_part(shard, start, stop):
        return weights[start:stop] - RATE * partial(shard, start, stop - start)

    def add_over_fsdp(terms):
        return [from_behind(term, "fsdp", away) for away, term in zip(range(1, shards), terms)]

    def u_of(chunk):
        start, stop = cuts[chunk], cuts[chunk + 1]
        total = base[0][start:stop] if stop <= split else base[1][start - split:stop - split]
        for term in arrived[chunk]:
            total = total - term.astype(jnp.float32) / scale
        return total

    def mixture(near, own, far):
        return (
            coeff[0:1] * (near.astype(jnp.float32) / scale)
            + coeff[1:2] * own
            + coeff[2:3] * (far.astype(jnp.float32) / scale)
        )

    def mix_into(out, chunk):
        value = mixture(near[chunk], u_of(chunk), far[chunk])
        return lax.dynamic_update_slice_in_dim(out, value, cuts[chunk], axis=0)

    near = {}
    far = {}
    mixed = 0
    out = jnp.zeros_like(weights)
    split = cuts[min(2, chunks)]
    terms = {0: for_others(0, cuts[1])}
    arrived = {0: add_over_fsdp(terms[0])}

    parts = [own_part(shard, main, rows)]
    parts += [-RATE * partial(owner(away), main, first) for away in range(1, shards)]
    parts = jnp.concatenate(parts, axis=0)
    parts, sent = lax.optimization_barrier((parts, (parts * scale).astype(WIRE)))
    far[-1] = swapped(sent, "blk", 1)
    near[-1] = swapped(sent, "blk", 0)

    if chunks > 1:
        parts, later = lax.optimization_barrier((parts, shard))
        rest = [
            (partial(owner(away, later), cuts[1], main - cuts[1]) * (RATE * scale)).astype(WIRE)
            for away in range(1, shards)
        ]
        for chunk in range(1, chunks):
            terms[chunk] = [term[cuts[chunk] - cuts[1]:cuts[chunk + 1] - cuts[1]] for term in rest]
        for chunk in range(1, min(AHEAD, chunks)):
            if chunk == 2:
                terms[chunk], near[-1] = lax.optimization_barrier((terms[chunk], near[-1]))
            arrived[chunk] = add_over_fsdp(terms[chunk])
    base = [own_part(shard, 0, split)]

    arrived[0], base, terms = lax.optimization_barrier((arrived[0], base, terms))
    for chunk in range(chunks):
        if chunk == 1:
            arrived[1], base = lax.optimization_barrier((arrived[1], base))
        if chunk >= 1:
            arrived[chunk], far[chunk - 2] = lax.optimization_barrier((arrived[chunk], far[chunk - 2]))
        arrived[chunk], near[chunk - 1] = lax.optimization_barrier((arrived[chunk], near[chunk - 1]))
        if mixed:
            arrived[chunk], out = lax.optimization_barrier((arrived[chunk], out))
        if chunk == 3:
            arrived[chunk], parts = lax.optimization_barrier((arrived[chunk], parts))
        sent = (u_of(chunk) * scale).astype(WIRE)
        sent, base, out, later = lax.optimization_barrier((sent, base, out, shard))
        if chunk == 0 and split < main:
            base.append(own_part(later, split, main))
        if chunk == middle:
            mix, parts, sent = lax.optimization_barrier((mix, parts, sent))
            coeff = lax.optimization_barrier(coefficients(mix))
            parts = mixture(near[-1], parts, far[-1])
            back = [
                (parts[away * first:(away + 1) * first] * scale).astype(WIRE) for away in range(1, shards)
            ]
            parts = parts[:first]
        after = chunk + AHEAD
        if after < chunks:
            terms[after], sent = lax.optimization_barrier((terms[after], sent))
            arrived[after] = add_over_fsdp(terms[after])
        if chunk == max(chunks - AHEAD, middle):
            back, sent = lax.optimization_barrier((back, sent))
            back = add_over_fsdp(back)
        far[chunk] = swapped(sent, "blk", 1)
        near[chunk] = swapped(sent, "blk", 0)
        if chunk >= MIXLAG:
            out = mix_into(out, mixed)
            mixed += 1

    for term in back:
        parts = parts + term.astype(jnp.float32) / scale
    out = lax.dynamic_update_slice_in_dim(out, parts, main, axis=0)
    for chunk in range(mixed, chunks):
        out = mix_into(out, chunk)
    return out[None]


def solution(mesh):
    return jax.shard_map(
        on_device,
        mesh=mesh,
        in_specs=(P("blk", "fsdp", None), P("blk", "fsdp", None), P("blk", "fsdp", None), P()),
        out_specs=P("blk", "fsdp", None),
        check_vma=False,
    )
```

```python
import math

import jax
import jax.numpy as jnp
from jax import lax
from jax.sharding import PartitionSpec as P

MIX_DENOM = 64
RATE = 0.03
LARGEST = 6.0
WIRE = jnp.float16
STEP = 256
FIRST = 128
AHEAD = 3
MIXLAG = 5


def from_behind(value, axis, steps):
    count = lax.axis_size(axis)
    pairs = [(source, (source + steps) % count) for source in range(count)]
    return lax.ppermute(value, axis, pairs)


def swapped(value, axis, first):
    count = lax.axis_size(axis)
    pairs = []
    for source in range(first, count, 2):
        partner = (source + 1) % count
        pairs += [(source, partner), (partner, source)]
    return lax.ppermute(value, axis, pairs)


def wire_scale(tokens):
    bound = LARGEST + RATE * LARGEST * LARGEST * tokens
    return 2.0 ** math.floor(math.log2(float(jnp.finfo(WIRE).max) / bound))


def on_device(params, inputs, cotangent, mix):
    weights = params[0]
    features = inputs[0]
    cot_local = cotangent[0]
    rows = weights.shape[0]
    shards = lax.axis_size("fsdp")
    scale = wire_scale(features.shape[0] * shards)
    replica = lax.axis_index("blk")
    shard = lax.axis_index("fsdp")
    def coefficients(mix):
        row = lax.dynamic_slice_in_dim(mix, replica, 1, axis=0).astype(jnp.float32)
        row = jnp.where(replica % 2 == 0, row[:, ::-1], row)
        column = jnp.reshape(row, (3, 1)) / MIX_DENOM
        return jnp.broadcast_to(column, (3, weights.shape[1]))

    first = min(FIRST, rows // 2)
    main = rows - first
    cuts = list(range(0, main, STEP)) + [main]
    chunks = len(cuts) - 1
    middle = min(1, chunks - 1)

    def owner(away, shard=shard):
        other = shard + away
        return jnp.where(other < shards, other, other - shards)

    def partial(owner, start, size):
        block = lax.dynamic_slice_in_dim(features, owner * rows + start, size, axis=1)
        return lax.dot_general(
            block, cot_local, (((0,), (0,)), ((), ())), preferred_element_type=jnp.float32
        )

    def for_others(start, stop):
        return [
            (partial(owner(away), start, stop - start) * (RATE * scale)).astype(WIRE)
            for away in range(1, shards)
        ]

    def own_part(shard, start, stop):
        return weights[start:stop] - RATE * partial(shard, start, stop - start)

    def add_over_fsdp(terms):
        return [from_behind(term, "fsdp", away) for away, term in zip(range(1, shards), terms)]

    def u_of(chunk):
        start, stop = cuts[chunk], cuts[chunk + 1]
        total = base[0][start:stop] if stop <= split else base[1][start - split:stop - split]
        for term in arrived[chunk]:
            total = total - term.astype(jnp.float32) / scale
        return total

    def mixture(near, own, far):
        return (
            coeff[0:1] * (near.astype(jnp.float32) / scale)
            + coeff[1:2] * own
            + coeff[2:3] * (far.astype(jnp.float32) / scale)
        )

    def mix_into(out, chunk):
        value = mixture(near[chunk], u_of(chunk), far[chunk])
        return lax.dynamic_update_slice_in_dim(out, value, cuts[chunk], axis=0)

    near = {}
    far = {}
    mixed = 0
    out = jnp.zeros_like(weights)
    split = cuts[min(3, chunks)]
    begun = min(2, chunks)
    made = for_others(0, cuts[begun])
    terms = {chunk: [term[cuts[chunk]:cuts[chunk + 1]] for term in made] for chunk in range(begun)}

    terms[0], later = lax.optimization_barrier((terms[0], shard))
    arrived = {0: add_over_fsdp(terms[0])}
    parts = [own_part(later, main, rows)]
    parts += [-RATE * partial(owner(away, later), main, first) for away in range(1, shards)]
    parts = jnp.concatenate(parts, axis=0)
    parts, sent = lax.optimization_barrier((parts, (parts * scale).astype(WIRE)))
    far[-1] = swapped(sent, "blk", 1)
    near[-1] = swapped(sent, "blk", 0)

    if begun > 1:
        arrived[1] = add_over_fsdp(terms[1])
    base = [own_part(shard, 0, split)]

    arrived[0], base, terms = lax.optimization_barrier((arrived[0], base, terms))
    for chunk in range(chunks):
        if chunk in (1, 3):
            arrived[chunk], base, terms = lax.optimization_barrier((arrived[chunk], base, terms))
        if chunk >= 1:
            arrived[chunk], far[chunk - 2] = lax.optimization_barrier((arrived[chunk], far[chunk - 2]))
        arrived[chunk], near[chunk - 1] = lax.optimization_barrier((arrived[chunk], near[chunk - 1]))
        if mixed:
            arrived[chunk], out = lax.optimization_barrier((arrived[chunk], out))
        if chunk == 3:
            arrived[chunk], parts = lax.optimization_barrier((arrived[chunk], parts))
        sent = (u_of(chunk) * scale).astype(WIRE)
        sent, base, out, later = lax.optimization_barrier((sent, base, out, shard))
        if chunk == 0 and begun < chunks:
            start = cuts[begun]
            rest = [
                (partial(owner(away, later), start, rows - start) * (RATE * scale)).astype(WIRE)
                for away in range(1, shards)
            ]
            for after in range(begun, chunks):
                terms[after] = [term[cuts[after] - start:cuts[after + 1] - start] for term in rest]
            for after in range(begun, min(AHEAD, chunks)):
                arrived[after] = add_over_fsdp(terms[after])
        if chunk == 2 and split < main:
            base.append(own_part(later, split, rows))
        if chunk == middle:
            mix, parts, sent = lax.optimization_barrier((mix, parts, sent))
            coeff = lax.optimization_barrier(coefficients(mix))
            parts = mixture(near[-1], parts, far[-1])
            back = [
                (parts[away * first:(away + 1) * first] * scale).astype(WIRE) for away in range(1, shards)
            ]
            parts = parts[:first]
        after = chunk + AHEAD
        if chunk > 0 and after < chunks:
            terms[after], sent = lax.optimization_barrier((terms[after], sent))
            arrived[after] = add_over_fsdp(terms[after])
        if chunk == max(chunks - AHEAD, middle):
            back, sent = lax.optimization_barrier((back, sent))
            back = add_over_fsdp(back)
        far[chunk] = swapped(sent, "blk", 1)
        near[chunk] = swapped(sent, "blk", 0)
        if chunk == 0 and after < chunks:
            terms[after], near[0] = lax.optimization_barrier((terms[after], near[0]))
            arrived[after] = add_over_fsdp(terms[after])
        if chunk >= MIXLAG:
            out = mix_into(out, mixed)
            mixed += 1

    for chunk in range(mixed, chunks):
        if chunk == chunks - 1:
            for term in back:
                parts = parts + term.astype(jnp.float32) / scale
            out = lax.dynamic_update_slice_in_dim(out, parts, main, axis=0)
        out = mix_into(out, chunk)
    return out[None]


def solution(mesh):
    return jax.shard_map(
        on_device,
        mesh=mesh,
        in_specs=(P("blk", "fsdp", None), P("blk", "fsdp", None), P("blk", "fsdp", None), P()),
        out_specs=P("blk", "fsdp", None),
        check_vma=False,
    )
```

```python
import math

import jax
import jax.numpy as jnp
from jax import lax
from jax.sharding import PartitionSpec as P

MIX_DENOM = 64
RATE = 0.03
LARGEST = 6.0
WIRE = jnp.float16
STEP = 256
FIRST = 128
AHEAD = 3
MIXLAG = 5


def from_behind(value, axis, steps):
    count = lax.axis_size(axis)
    pairs = [(source, (source + steps) % count) for source in range(count)]
    return lax.ppermute(value, axis, pairs)


def swapped(value, axis, first):
    count = lax.axis_size(axis)
    pairs = []
    for source in range(first, count, 2):
        partner = (source + 1) % count
        pairs += [(source, partner), (partner, source)]
    return lax.ppermute(value, axis, pairs)


def wire_scale(tokens):
    bound = LARGEST + RATE * LARGEST * LARGEST * tokens
    return 2.0 ** math.floor(math.log2(float(jnp.finfo(WIRE).max) / bound))


def on_device(params, inputs, cotangent, mix):
    weights = params[0]
    features = inputs[0]
    cot_local = cotangent[0]
    rows = weights.shape[0]
    shards = lax.axis_size("fsdp")
    scale = wire_scale(features.shape[0] * shards)
    replica = lax.axis_index("blk")
    shard = lax.axis_index("fsdp")
    def coefficients(mix):
        row = lax.dynamic_slice_in_dim(mix, replica, 1, axis=0).astype(jnp.float32)
        row = jnp.where(replica % 2 == 0, row[:, ::-1], row)
        column = jnp.reshape(row, (3, 1)) / MIX_DENOM
        return jnp.broadcast_to(column, (3, weights.shape[1]))

    first = min(FIRST, rows // 2)
    main = rows - first
    cuts = list(range(0, main, STEP)) + [main]
    chunks = len(cuts) - 1
    middle = min(1, chunks - 1)

    def owner(away, shard=shard):
        other = shard + away
        return jnp.where(other < shards, other, other - shards)

    def partial(owner, start, size):
        block = lax.dynamic_slice_in_dim(features, owner * rows + start, size, axis=1)
        return lax.dot_general(
            block, cot_local, (((0,), (0,)), ((), ())), preferred_element_type=jnp.float32
        )

    def for_others(start, stop):
        return [
            (partial(owner(away), start, stop - start) * (RATE * scale)).astype(WIRE)
            for away in range(1, shards)
        ]

    def own_part(shard, start, stop):
        return weights[start:stop] - RATE * partial(shard, start, stop - start)

    def add_over_fsdp(terms):
        return [from_behind(term, "fsdp", away) for away, term in zip(range(1, shards), terms)]

    def u_of(chunk):
        start, stop = cuts[chunk], cuts[chunk + 1]
        total = base[0][start:stop] if stop <= split else base[1][start - split:stop - split]
        for term in arrived[chunk]:
            total = total - term.astype(jnp.float32) / scale
        return total

    def mixture(near, own, far):
        return (
            coeff[0:1] * (near.astype(jnp.float32) / scale)
            + coeff[1:2] * own
            + coeff[2:3] * (far.astype(jnp.float32) / scale)
        )

    def mix_into(out, chunk):
        value = mixture(near[chunk], u_of(chunk), far[chunk])
        return lax.dynamic_update_slice_in_dim(out, value, cuts[chunk], axis=0)

    near = {}
    far = {}
    mixed = 0
    out = jnp.zeros_like(weights)
    split = cuts[min(3, chunks)]
    begun = min(3, chunks)
    made = for_others(0, cuts[begun])
    terms = {chunk: [term[cuts[chunk]:cuts[chunk + 1]] for term in made] for chunk in range(begun)}

    terms[0], later = lax.optimization_barrier((terms[0], shard))
    arrived = {0: add_over_fsdp(terms[0])}
    parts = [own_part(later, main, rows)]
    parts += [-RATE * partial(owner(away, later), main, first) for away in range(1, shards)]
    parts = jnp.concatenate(parts, axis=0)
    parts, sent = lax.optimization_barrier((parts, (parts * scale).astype(WIRE)))
    far[-1] = swapped(sent, "blk", 1)
    near[-1] = swapped(sent, "blk", 0)

    for chunk in range(1, begun):
        arrived[chunk] = add_over_fsdp(terms[chunk])
    base = [own_part(shard, 0, split)]

    arrived[0], base, terms = lax.optimization_barrier((arrived[0], base, terms))
    for chunk in range(chunks):
        if chunk in (1, 3):
            arrived[chunk], base, terms = lax.optimization_barrier((arrived[chunk], base, terms))
        if chunk >= 1:
            arrived[chunk], far[chunk - 2] = lax.optimization_barrier((arrived[chunk], far[chunk - 2]))
        arrived[chunk], near[chunk - 1] = lax.optimization_barrier((arrived[chunk], near[chunk - 1]))
        if mixed:
            arrived[chunk], out = lax.optimization_barrier((arrived[chunk], out))
        if chunk == 3:
            arrived[chunk], parts = lax.optimization_barrier((arrived[chunk], parts))
        sent = (u_of(chunk) * scale).astype(WIRE)
        sent, base, out, later = lax.optimization_barrier((sent, base, out, shard))
        if chunk == 0 and begun < chunks:
            start = cuts[begun]
            rest = [
                (partial(owner(away, later), start, rows - start) * (RATE * scale)).astype(WIRE)
                for away in range(1, shards)
            ]
            for after in range(begun, chunks):
                terms[after] = [term[cuts[after] - start:cuts[after + 1] - start] for term in rest]
            for after in range(begun, min(AHEAD, chunks)):
                arrived[after] = add_over_fsdp(terms[after])
        if chunk == 2 and split < main:
            base.append(own_part(later, split, rows))
        if chunk == middle:
            mix, parts, sent = lax.optimization_barrier((mix, parts, sent))
            coeff = lax.optimization_barrier(coefficients(mix))
            parts = mixture(near[-1], parts, far[-1])
            back = [
                (parts[away * first:(away + 1) * first] * scale).astype(WIRE) for away in range(1, shards)
            ]
            parts = parts[:first]
        after = chunk + AHEAD
        if chunk > 0 and after < chunks:
            terms[after], sent = lax.optimization_barrier((terms[after], sent))
            arrived[after] = add_over_fsdp(terms[after])
        if chunk == max(chunks - AHEAD, middle):
            back, sent = lax.optimization_barrier((back, sent))
            back = add_over_fsdp(back)
        far[chunk] = swapped(sent, "blk", 1)
        near[chunk] = swapped(sent, "blk", 0)
        if chunk == 0 and after < chunks:
            terms[after], near[0] = lax.optimization_barrier((terms[after], near[0]))
            arrived[after] = add_over_fsdp(terms[after])
        if chunk >= MIXLAG:
            out = mix_into(out, mixed)
            mixed += 1

    for chunk in range(mixed, chunks):
        if chunk == chunks - 1:
            for term in back:
                parts = parts + term.astype(jnp.float32) / scale
            out = lax.dynamic_update_slice_in_dim(out, parts, main, axis=0)
        out = mix_into(out, chunk)
    return out[None]


def solution(mesh):
    return jax.shard_map(
        on_device,
        mesh=mesh,
        in_specs=(P("blk", "fsdp", None), P("blk", "fsdp", None), P("blk", "fsdp", None), P()),
        out_specs=P("blk", "fsdp", None),
        check_vma=False,
    )
```

```python
import math

import jax
import jax.numpy as jnp
from jax import lax
from jax.sharding import PartitionSpec as P

MIX_DENOM = 64
RATE = 0.03
LARGEST = 6.0
WIRE = jnp.float16
STEP = 256
FIRST = 128
AHEAD = 3
MIXLAG = 5


def from_behind(value, axis, steps):
    count = lax.axis_size(axis)
    pairs = [(source, (source + steps) % count) for source in range(count)]
    return lax.ppermute(value, axis, pairs)


def swapped(value, axis, first):
    count = lax.axis_size(axis)
    pairs = []
    for source in range(first, count, 2):
        partner = (source + 1) % count
        pairs += [(source, partner), (partner, source)]
    return lax.ppermute(value, axis, pairs)


def wire_scale(tokens):
    bound = LARGEST + RATE * LARGEST * LARGEST * tokens
    return 2.0 ** math.floor(math.log2(float(jnp.finfo(WIRE).max) / bound))


def on_device(params, inputs, cotangent, mix):
    weights = params[0]
    features = inputs[0]
    cot_local = cotangent[0]
    rows = weights.shape[0]
    shards = lax.axis_size("fsdp")
    scale = wire_scale(features.shape[0] * shards)
    replica = lax.axis_index("blk")
    shard = lax.axis_index("fsdp")
    def coefficients(mix):
        row = lax.dynamic_slice_in_dim(mix, replica, 1, axis=0).astype(jnp.float32)
        row = jnp.where(replica % 2 == 0, row[:, ::-1], row)
        column = jnp.reshape(row, (3, 1)) / MIX_DENOM
        return jnp.broadcast_to(column, (3, weights.shape[1]))

    first = min(FIRST, rows // 2)
    main = rows - first
    cuts = list(range(0, main, STEP)) + [main]
    chunks = len(cuts) - 1
    middle = min(3, chunks - 1)

    def owner(away, shard=shard):
        other = shard + away
        return jnp.where(other < shards, other, other - shards)

    def partial(owner, start, size):
        block = lax.dynamic_slice_in_dim(features, owner * rows + start, size, axis=1)
        return lax.dot_general(
            block, cot_local, (((0,), (0,)), ((), ())), preferred_element_type=jnp.float32
        )

    def for_others(start, stop):
        return [
            (partial(owner(away), start, stop - start) * (RATE * scale)).astype(WIRE)
            for away in range(1, shards)
        ]

    def own_part(shard, start, stop):
        return weights[start:stop] - RATE * partial(shard, start, stop - start)

    def add_over_fsdp(terms):
        return [from_behind(term, "fsdp", away) for away, term in zip(range(1, shards), terms)]

    def u_of(chunk):
        start, stop = cuts[chunk], cuts[chunk + 1]
        total = base[0][start:stop] if stop <= split else base[1][start - split:stop - split]
        for term in arrived[chunk]:
            total = total - term.astype(jnp.float32) / scale
        return total

    def mixture(near, own, far):
        return (
            coeff[0:1] * (near.astype(jnp.float32) / scale)
            + coeff[1:2] * own
            + coeff[2:3] * (far.astype(jnp.float32) / scale)
        )

    def mix_into(out, chunk):
        value = mixture(near[chunk], u_of(chunk), far[chunk])
        return lax.dynamic_update_slice_in_dim(out, value, cuts[chunk], axis=0)

    near = {}
    far = {}
    mixed = 0
    out = jnp.zeros_like(weights)
    split = cuts[min(3, chunks)]
    begun = min(3, chunks)
    made = for_others(0, cuts[begun])
    terms = {chunk: [term[cuts[chunk]:cuts[chunk + 1]] for term in made] for chunk in range(begun)}

    terms[0], later = lax.optimization_barrier((terms[0], shard))
    arrived = {0: add_over_fsdp(terms[0])}
    parts = [own_part(later, main, rows)]
    parts += [-RATE * partial(owner(away, later), main, first) for away in range(1, shards)]
    parts = jnp.concatenate(parts, axis=0)
    parts, sent = lax.optimization_barrier((parts, (parts * scale).astype(WIRE)))
    far[-1] = swapped(sent, "blk", 1)
    near[-1] = swapped(sent, "blk", 0)

    for chunk in range(1, begun):
        arrived[chunk] = add_over_fsdp(terms[chunk])
    base = [own_part(shard, 0, split)]

    arrived[0], base, terms = lax.optimization_barrier((arrived[0], base, terms))
    for chunk in range(chunks):
        if chunk in (1, 3):
            arrived[chunk], base, terms = lax.optimization_barrier((arrived[chunk], base, terms))
        if chunk >= 1:
            arrived[chunk], far[chunk - 2] = lax.optimization_barrier((arrived[chunk], far[chunk - 2]))
        arrived[chunk], near[chunk - 1] = lax.optimization_barrier((arrived[chunk], near[chunk - 1]))
        if mixed:
            arrived[chunk], out = lax.optimization_barrier((arrived[chunk], out))
        if chunk == middle + 2:
            arrived[chunk], parts = lax.optimization_barrier((arrived[chunk], parts))
        sent = (u_of(chunk) * scale).astype(WIRE)
        sent, base, out, later = lax.optimization_barrier((sent, base, out, shard))
        if chunk == 0 and begun < chunks:
            start = cuts[begun]
            rest = [
                (partial(owner(away, later), start, rows - start) * (RATE * scale)).astype(WIRE)
                for away in range(1, shards)
            ]
            for after in range(begun, chunks):
                terms[after] = [term[cuts[after] - start:cuts[after + 1] - start] for term in rest]
            for after in range(begun, min(AHEAD, chunks)):
                arrived[after] = add_over_fsdp(terms[after])
        if chunk == 2 and split < main:
            base.append(own_part(later, split, rows))
        if chunk == middle:
            mix, parts, sent = lax.optimization_barrier((mix, parts, sent))
            coeff = lax.optimization_barrier(coefficients(mix))
            parts = mixture(near[-1], parts, far[-1])
            back = [
                (parts[away * first:(away + 1) * first] * scale).astype(WIRE) for away in range(1, shards)
            ]
            parts = parts[:first]
        after = chunk + AHEAD
        if chunk > 0 and after < chunks:
            terms[after], sent = lax.optimization_barrier((terms[after], sent))
            arrived[after] = add_over_fsdp(terms[after])
        if chunk == max(chunks - AHEAD, middle):
            back, sent = lax.optimization_barrier((back, sent))
            back = add_over_fsdp(back)
        far[chunk] = swapped(sent, "blk", 1)
        near[chunk] = swapped(sent, "blk", 0)
        if chunk == 0 and after < chunks:
            terms[after], near[0] = lax.optimization_barrier((terms[after], near[0]))
            arrived[after] = add_over_fsdp(terms[after])
        if chunk >= MIXLAG:
            out = mix_into(out, mixed)
            mixed += 1

    for chunk in range(mixed, chunks):
        if chunk == chunks - 1:
            for term in back:
                parts = parts + term.astype(jnp.float32) / scale
            out = lax.dynamic_update_slice_in_dim(out, parts, main, axis=0)
        out = mix_into(out, chunk)
    return out[None]


def solution(mesh):
    return jax.shard_map(
        on_device,
        mesh=mesh,
        in_specs=(P("blk", "fsdp", None), P("blk", "fsdp", None), P("blk", "fsdp", None), P()),
        out_specs=P("blk", "fsdp", None),
        check_vma=False,
    )
```

```python
import math

import jax
import jax.numpy as jnp
from jax import lax
from jax.sharding import PartitionSpec as P

MIX_DENOM = 64
RATE = 0.03
LARGEST = 6.0
WIRE = jnp.float16
STEP = 256
FIRST = 128
AHEAD = 3
MIXLAG = 3


def from_behind(value, axis, steps):
    count = lax.axis_size(axis)
    pairs = [(source, (source + steps) % count) for source in range(count)]
    return lax.ppermute(value, axis, pairs)


def swapped(value, axis, first):
    count = lax.axis_size(axis)
    pairs = []
    for source in range(first, count, 2):
        partner = (source + 1) % count
        pairs += [(source, partner), (partner, source)]
    return lax.ppermute(value, axis, pairs)


def wire_scale(tokens):
    bound = LARGEST + RATE * LARGEST * LARGEST * tokens
    return 2.0 ** math.floor(math.log2(float(jnp.finfo(WIRE).max) / bound))


def on_device(params, inputs, cotangent, mix):
    weights = params[0]
    features = inputs[0]
    cot_local = cotangent[0]
    rows = weights.shape[0]
    shards = lax.axis_size("fsdp")
    scale = wire_scale(features.shape[0] * shards)
    replica = lax.axis_index("blk")
    shard = lax.axis_index("fsdp")
    def coefficients(mix):
        row = lax.dynamic_slice_in_dim(mix, replica, 1, axis=0).astype(jnp.float32)
        row = jnp.where(replica % 2 == 0, row[:, ::-1], row)
        column = jnp.reshape(row, (3, 1)) / MIX_DENOM
        return jnp.broadcast_to(column, (3, weights.shape[1]))

    first = min(FIRST, rows // 2)
    main = rows - first
    cuts = list(range(0, main, STEP)) + [main]
    chunks = len(cuts) - 1
    middle = min(2, chunks - 1)

    def owner(away, shard=shard):
        other = shard + away
        return jnp.where(other < shards, other, other - shards)

    def partial(owner, start, size):
        block = lax.dynamic_slice_in_dim(features, owner * rows + start, size, axis=1)
        return lax.dot_general(
            block, cot_local, (((0,), (0,)), ((), ())), preferred_element_type=jnp.float32
        )

    def for_others(start, stop):
        return [
            (partial(owner(away), start, stop - start) * (RATE * scale)).astype(WIRE)
            for away in range(1, shards)
        ]

    def own_part(shard, start, stop):
        return weights[start:stop] - RATE * partial(shard, start, stop - start)

    def add_over_fsdp(terms):
        return [from_behind(term, "fsdp", away) for away, term in zip(range(1, shards), terms)]

    def u_of(chunk):
        start, stop = cuts[chunk], cuts[chunk + 1]
        total = base[0][start:stop] if stop <= split else base[1][start - split:stop - split]
        for term in arrived[chunk]:
            total = total - term.astype(jnp.float32) / scale
        return total

    def mixture(near, own, far):
        return (
            coeff[0:1] * (near.astype(jnp.float32) / scale)
            + coeff[1:2] * own
            + coeff[2:3] * (far.astype(jnp.float32) / scale)
        )

    def mix_into(out, chunk):
        value = mixture(near[chunk], u_of(chunk), far[chunk])
        return lax.dynamic_update_slice_in_dim(out, value, cuts[chunk], axis=0)

    near = {}
    far = {}
    mixed = 0
    out = jnp.zeros_like(weights)
    split = cuts[min(3, chunks)]
    begun = min(3, chunks)
    made = for_others(0, cuts[begun])
    terms = {chunk: [term[cuts[chunk]:cuts[chunk + 1]] for term in made] for chunk in range(begun)}

    terms[0], later = lax.optimization_barrier((terms[0], shard))
    arrived = {0: add_over_fsdp(terms[0])}
    parts = [own_part(later, main, rows)]
    parts += [-RATE * partial(owner(away, later), main, first) for away in range(1, shards)]
    parts = jnp.concatenate(parts, axis=0)
    parts, sent = lax.optimization_barrier((parts, (parts * scale).astype(WIRE)))
    far[-1] = swapped(sent, "blk", 1)
    near[-1] = swapped(sent, "blk", 0)

    for chunk in range(1, begun):
        arrived[chunk] = add_over_fsdp(terms[chunk])
    base = [own_part(shard, 0, split)]

    arrived[0], base, terms = lax.optimization_barrier((arrived[0], base, terms))
    for chunk in range(chunks):
        if chunk in (1, 3):
            arrived[chunk], base, terms = lax.optimization_barrier((arrived[chunk], base, terms))
        if chunk >= 1:
            arrived[chunk], far[chunk - 2] = lax.optimization_barrier((arrived[chunk], far[chunk - 2]))
        arrived[chunk], near[chunk - 1] = lax.optimization_barrier((arrived[chunk], near[chunk - 1]))
        if mixed:
            arrived[chunk], out = lax.optimization_barrier((arrived[chunk], out))
        if chunk == middle + 2:
            arrived[chunk], parts = lax.optimization_barrier((arrived[chunk], parts))
        sent = (u_of(chunk) * scale).astype(WIRE)
        sent, base, out, later = lax.optimization_barrier((sent, base, out, shard))
        if chunk == 0 and begun < chunks:
            start = cuts[begun]
            rest = [
                (partial(owner(away, later), start, rows - start) * (RATE * scale)).astype(WIRE)
                for away in range(1, shards)
            ]
            for after in range(begun, chunks):
                terms[after] = [term[cuts[after] - start:cuts[after + 1] - start] for term in rest]
            for after in range(begun, min(AHEAD, chunks)):
                arrived[after] = add_over_fsdp(terms[after])
        if chunk == 2 and split < main:
            base.append(own_part(later, split, rows))
        if chunk == middle:
            mix, parts, sent = lax.optimization_barrier((mix, parts, sent))
            coeff = lax.optimization_barrier(coefficients(mix))
            parts = mixture(near[-1], parts, far[-1])
            back = [
                (parts[away * first:(away + 1) * first] * scale).astype(WIRE) for away in range(1, shards)
            ]
            parts = parts[:first]
        after = chunk + AHEAD
        if chunk > 0 and after < chunks:
            terms[after], sent = lax.optimization_barrier((terms[after], sent))
            arrived[after] = add_over_fsdp(terms[after])
        if chunk == max(chunks - AHEAD, middle):
            back, sent = lax.optimization_barrier((back, sent))
            back = add_over_fsdp(back)
        far[chunk] = swapped(sent, "blk", 1)
        near[chunk] = swapped(sent, "blk", 0)
        if chunk == 0 and after < chunks:
            terms[after], near[0] = lax.optimization_barrier((terms[after], near[0]))
            arrived[after] = add_over_fsdp(terms[after])
        if chunk >= MIXLAG:
            out = mix_into(out, mixed)
            mixed += 1

    for chunk in range(mixed, chunks):
        if chunk == chunks - 1:
            for term in back:
                parts = parts + term.astype(jnp.float32) / scale
            out = lax.dynamic_update_slice_in_dim(out, parts, main, axis=0)
        out = mix_into(out, chunk)
    return out[None]


def solution(mesh):
    return jax.shard_map(
        on_device,
        mesh=mesh,
        in_specs=(P("blk", "fsdp", None), P("blk", "fsdp", None), P("blk", "fsdp", None), P()),
        out_specs=P("blk", "fsdp", None),
        check_vma=False,
    )
```

```python
import math

import jax
import jax.numpy as jnp
from jax import lax
from jax.sharding import PartitionSpec as P

MIX_DENOM = 64
RATE = 0.03
LARGEST = 6.0
WIRE = jnp.float16
STEP = 256
FIRST = 128
AHEAD = 3
MIXLAG = 3


def from_behind(value, axis, steps):
    count = lax.axis_size(axis)
    pairs = [(source, (source + steps) % count) for source in range(count)]
    return lax.ppermute(value, axis, pairs)


def swapped(value, axis, first):
    count = lax.axis_size(axis)
    pairs = []
    for source in range(first, count, 2):
        partner = (source + 1) % count
        pairs += [(source, partner), (partner, source)]
    return lax.ppermute(value, axis, pairs)


def wire_scale(tokens):
    bound = LARGEST + RATE * LARGEST * LARGEST * tokens
    return 2.0 ** math.floor(math.log2(float(jnp.finfo(WIRE).max) / bound))


def on_device(params, inputs, cotangent, mix):
    weights = params[0]
    features = inputs[0]
    cot_local = cotangent[0]
    rows = weights.shape[0]
    shards = lax.axis_size("fsdp")
    scale = wire_scale(features.shape[0] * shards)
    replica = lax.axis_index("blk")
    shard = lax.axis_index("fsdp")
    def coefficients(mix):
        row = lax.dynamic_slice_in_dim(mix, replica, 1, axis=0).astype(jnp.float32)
        row = jnp.where(replica % 2 == 0, row[:, ::-1], row)
        column = jnp.reshape(row, (3, 1)) / MIX_DENOM
        return jnp.broadcast_to(column, (3, weights.shape[1]))

    first = min(FIRST, rows // 2)
    main = rows - first
    cuts = list(range(0, main, STEP)) + [main]
    chunks = len(cuts) - 1
    middle = min(2, chunks - 1)

    def owner(away, shard=shard):
        other = shard + away
        return jnp.where(other < shards, other, other - shards)

    def partial(owner, start, size):
        block = lax.dynamic_slice_in_dim(features, owner * rows + start, size, axis=1)
        return lax.dot_general(
            block, cot_local, (((0,), (0,)), ((), ())), preferred_element_type=jnp.float32
        )

    def for_others(start, stop):
        return [
            (partial(owner(away), start, stop - start) * (RATE * scale)).astype(WIRE)
            for away in range(1, shards)
        ]

    def own_part(shard, start, stop):
        return weights[start:stop] - RATE * partial(shard, start, stop - start)

    def add_over_fsdp(terms):
        return [from_behind(term, "fsdp", away) for away, term in zip(range(1, shards), terms)]

    def u_of(chunk):
        start, stop = cuts[chunk], cuts[chunk + 1]
        total = base[0][start:stop] if stop <= split else base[1][start - split:stop - split]
        for term in arrived[chunk]:
            total = total - term.astype(jnp.float32) / scale
        return total

    def mixture(near, own, far):
        return (
            coeff[0:1] * (near.astype(jnp.float32) / scale)
            + coeff[1:2] * own
            + coeff[2:3] * (far.astype(jnp.float32) / scale)
        )

    def mix_into(out, chunk):
        value = mixture(near[chunk], u_of(chunk), far[chunk])
        return lax.dynamic_update_slice_in_dim(out, value, cuts[chunk], axis=0)

    near = {}
    far = {}
    mixed = 0
    out = jnp.zeros_like(weights)
    split = cuts[min(3, chunks)]
    begun = min(3, chunks)
    terms = {0: for_others(0, cuts[1])}

    terms[0], later = lax.optimization_barrier((terms[0], shard))
    arrived = {0: add_over_fsdp(terms[0])}
    parts = [own_part(later, main, rows)]
    parts += [-RATE * partial(owner(away, later), main, first) for away in range(1, shards)]
    parts = jnp.concatenate(parts, axis=0)
    parts, sent = lax.optimization_barrier((parts, (parts * scale).astype(WIRE)))
    far[-1] = swapped(sent, "blk", 1)
    near[-1] = swapped(sent, "blk", 0)

    if begun > 1:
        parts, later = lax.optimization_barrier((parts, shard))
        size = cuts[begun] - cuts[1]
        made = [
            (partial(owner(away, later), cuts[1], size) * (RATE * scale)).astype(WIRE)
            for away in range(1, shards)
        ]
        for chunk in range(1, begun):
            terms[chunk] = [term[cuts[chunk] - cuts[1]:cuts[chunk + 1] - cuts[1]] for term in made]
            arrived[chunk] = add_over_fsdp(terms[chunk])
    base = [own_part(shard, 0, split)]

    arrived[0], base, terms = lax.optimization_barrier((arrived[0], base, terms))
    for chunk in range(chunks):
        if chunk in (1, 3):
            arrived[chunk], base, terms = lax.optimization_barrier((arrived[chunk], base, terms))
        if chunk >= 1:
            arrived[chunk], far[chunk - 2] = lax.optimization_barrier((arrived[chunk], far[chunk - 2]))
        arrived[chunk], near[chunk - 1] = lax.optimization_barrier((arrived[chunk], near[chunk - 1]))
        if mixed:
            arrived[chunk], out = lax.optimization_barrier((arrived[chunk], out))
        if chunk == middle + 2:
            arrived[chunk], parts = lax.optimization_barrier((arrived[chunk], parts))
        sent = (u_of(chunk) * scale).astype(WIRE)
        sent, base, out, later = lax.optimization_barrier((sent, base, out, shard))
        if chunk == 0 and begun < chunks:
            start = cuts[begun]
            rest = [
                (partial(owner(away, later), start, rows - start) * (RATE * scale)).astype(WIRE)
                for away in range(1, shards)
            ]
            for after in range(begun, chunks):
                terms[after] = [term[cuts[after] - start:cuts[after + 1] - start] for term in rest]
            for after in range(begun, min(AHEAD, chunks)):
                arrived[after] = add_over_fsdp(terms[after])
        if chunk == 2 and split < main:
            base.append(own_part(later, split, rows))
        if chunk == middle:
            mix, parts, sent = lax.optimization_barrier((mix, parts, sent))
            coeff = lax.optimization_barrier(coefficients(mix))
            parts = mixture(near[-1], parts, far[-1])
            back = [
                (parts[away * first:(away + 1) * first] * scale).astype(WIRE) for away in range(1, shards)
            ]
            parts = parts[:first]
        after = chunk + AHEAD
        if chunk > 0 and after < chunks:
            terms[after], sent = lax.optimization_barrier((terms[after], sent))
            arrived[after] = add_over_fsdp(terms[after])
        if chunk == max(chunks - AHEAD, middle):
            back, sent = lax.optimization_barrier((back, sent))
            back = add_over_fsdp(back)
        far[chunk] = swapped(sent, "blk", 1)
        near[chunk] = swapped(sent, "blk", 0)
        if chunk == 0 and after < chunks:
            terms[after], near[0] = lax.optimization_barrier((terms[after], near[0]))
            arrived[after] = add_over_fsdp(terms[after])
        if chunk >= MIXLAG:
            out = mix_into(out, mixed)
            mixed += 1

    for chunk in range(mixed, chunks):
        if chunk == chunks - 1:
            for term in back:
                parts = parts + term.astype(jnp.float32) / scale
            out = lax.dynamic_update_slice_in_dim(out, parts, main, axis=0)
        out = mix_into(out, chunk)
    return out[None]


def solution(mesh):
    return jax.shard_map(
        on_device,
        mesh=mesh,
        in_specs=(P("blk", "fsdp", None), P("blk", "fsdp", None), P("blk", "fsdp", None), P()),
        out_specs=P("blk", "fsdp", None),
        check_vma=False,
    )
```

```python
import math

import jax
import jax.numpy as jnp
from jax import lax
from jax.sharding import PartitionSpec as P

MIX_DENOM = 64
RATE = 0.03
LARGEST = 6.0
WIRE = jnp.float16
STEP = 256
FIRST = 256
AHEAD = 3
MIXLAG = 5


def from_behind(value, axis, steps):
    count = lax.axis_size(axis)
    pairs = [(source, (source + steps) % count) for source in range(count)]
    return lax.ppermute(value, axis, pairs)


def swapped(value, axis, first):
    count = lax.axis_size(axis)
    pairs = []
    for source in range(first, count, 2):
        partner = (source + 1) % count
        pairs += [(source, partner), (partner, source)]
    return lax.ppermute(value, axis, pairs)


def wire_scale(tokens):
    bound = LARGEST + RATE * LARGEST * LARGEST * tokens
    return 2.0 ** math.floor(math.log2(float(jnp.finfo(WIRE).max) / bound))


def on_device(params, inputs, cotangent, mix):
    weights = params[0]
    features = inputs[0]
    cot_local = cotangent[0]
    rows = weights.shape[0]
    shards = lax.axis_size("fsdp")
    scale = wire_scale(features.shape[0] * shards)
    replica = lax.axis_index("blk")
    shard = lax.axis_index("fsdp")
    def coefficients(mix):
        row = lax.dynamic_slice_in_dim(mix, replica, 1, axis=0).astype(jnp.float32)
        row = jnp.where(replica % 2 == 0, row[:, ::-1], row)
        column = jnp.reshape(row, (3, 1)) / MIX_DENOM
        return jnp.broadcast_to(column, (3, weights.shape[1]))

    first = min(FIRST, rows // 2)
    main = rows - first
    cuts = list(range(0, main, STEP)) + [main]
    chunks = len(cuts) - 1
    middle = min(1, chunks - 1)

    def owner(away, shard=shard):
        other = shard + away
        return jnp.where(other < shards, other, other - shards)

    def partial(owner, start, size):
        block = lax.dynamic_slice_in_dim(features, owner * rows + start, size, axis=1)
        return lax.dot_general(
            block, cot_local, (((0,), (0,)), ((), ())), preferred_element_type=jnp.float32
        )

    def for_others(start, stop):
        return [
            (partial(owner(away), start, stop - start) * (RATE * scale)).astype(WIRE)
            for away in range(1, shards)
        ]

    def own_part(shard, start, stop):
        return weights[start:stop] - RATE * partial(shard, start, stop - start)

    def add_over_fsdp(terms):
        return [from_behind(term, "fsdp", away) for away, term in zip(range(1, shards), terms)]

    def u_of(chunk):
        start, stop = cuts[chunk], cuts[chunk + 1]
        total = base[0][start:stop] if stop <= split else base[1][start - split:stop - split]
        for term in arrived[chunk]:
            total = total - term.astype(jnp.float32) / scale
        return total

    def mixture(near, own, far):
        return (
            coeff[0:1] * (near.astype(jnp.float32) / scale)
            + coeff[1:2] * own
            + coeff[2:3] * (far.astype(jnp.float32) / scale)
        )

    def mix_into(out, chunk):
        value = mixture(near[chunk], u_of(chunk), far[chunk])
        return lax.dynamic_update_slice_in_dim(out, value, cuts[chunk], axis=0)

    near = {}
    far = {}
    mixed = 0
    out = jnp.zeros_like(weights)
    split = cuts[min(2, chunks)]
    terms = {0: for_others(0, cuts[1])}
    arrived = {0: add_over_fsdp(terms[0])}

    parts = [own_part(shard, main, rows)]
    parts += [-RATE * partial(owner(away), main, first) for away in range(1, shards)]
    parts = jnp.concatenate(parts, axis=0)
    parts, sent = lax.optimization_barrier((parts, (parts * scale).astype(WIRE)))
    far[-1] = swapped(sent, "blk", 1)
    near[-1] = swapped(sent, "blk", 0)

    if chunks > 1:
        parts, later = lax.optimization_barrier((parts, shard))
        rest = [
            (partial(owner(away, later), cuts[1], main - cuts[1]) * (RATE * scale)).astype(WIRE)
            for away in range(1, shards)
        ]
        for chunk in range(1, chunks):
            terms[chunk] = [term[cuts[chunk] - cuts[1]:cuts[chunk + 1] - cuts[1]] for term in rest]
        for chunk in range(1, min(AHEAD, chunks)):
            if chunk == 2:
                terms[chunk], near[-1] = lax.optimization_barrier((terms[chunk], near[-1]))
            arrived[chunk] = add_over_fsdp(terms[chunk])
    base = [own_part(shard, 0, split)]

    arrived[0], base, terms = lax.optimization_barrier((arrived[0], base, terms))
    for chunk in range(chunks):
        if chunk == 1:
            arrived[1], base = lax.optimization_barrier((arrived[1], base))
        if chunk >= 1:
            arrived[chunk], far[chunk - 2] = lax.optimization_barrier((arrived[chunk], far[chunk - 2]))
        arrived[chunk], near[chunk - 1] = lax.optimization_barrier((arrived[chunk], near[chunk - 1]))
        if mixed:
            arrived[chunk], out = lax.optimization_barrier((arrived[chunk], out))
        if chunk == 3:
            arrived[chunk], parts = lax.optimization_barrier((arrived[chunk], parts))
        sent = (u_of(chunk) * scale).astype(WIRE)
        sent, base, out, later = lax.optimization_barrier((sent, base, out, shard))
        if chunk == 0 and split < main:
            base.append(own_part(later, split, main))
        if chunk == middle:
            mix, parts, sent = lax.optimization_barrier((mix, parts, sent))
            coeff = lax.optimization_barrier(coefficients(mix))
            parts = mixture(near[-1], parts, far[-1])
            back = [
                (parts[away * first:(away + 1) * first] * scale).astype(WIRE) for away in range(1, shards)
            ]
            parts = parts[:first]
        after = chunk + AHEAD
        if after < chunks:
            terms[after], sent = lax.optimization_barrier((terms[after], sent))
            arrived[after] = add_over_fsdp(terms[after])
        if chunk == max(chunks - AHEAD, middle):
            back, sent = lax.optimization_barrier((back, sent))
            back = add_over_fsdp(back)
        far[chunk] = swapped(sent, "blk", 1)
        near[chunk] = swapped(sent, "blk", 0)
        if chunk >= MIXLAG:
            out = mix_into(out, mixed)
            mixed += 1

    for term in back:
        parts = parts + term.astype(jnp.float32) / scale
    out = lax.dynamic_update_slice_in_dim(out, parts, main, axis=0)
    for chunk in range(mixed, chunks):
        out = mix_into(out, chunk)
    return out[None]


def solution(mesh):
    return jax.shard_map(
        on_device,
        mesh=mesh,
        in_specs=(P("blk", "fsdp", None), P("blk", "fsdp", None), P("blk", "fsdp", None), P()),
        out_specs=P("blk", "fsdp", None),
        check_vma=False,
    )
```

```python
import math

import jax
import jax.numpy as jnp
from jax import lax
from jax.sharding import PartitionSpec as P

MIX_DENOM = 64
RATE = 0.03
LARGEST = 6.0
WIRE = jnp.float16
STEP = 256
FIRST = 256
AHEAD = 3
MIXLAG = 4


def from_behind(value, axis, steps):
    count = lax.axis_size(axis)
    pairs = [(source, (source + steps) % count) for source in range(count)]
    return lax.ppermute(value, axis, pairs)


def swapped(value, axis, first):
    count = lax.axis_size(axis)
    pairs = []
    for source in range(first, count, 2):
        partner = (source + 1) % count
        pairs += [(source, partner), (partner, source)]
    return lax.ppermute(value, axis, pairs)


def wire_scale(tokens):
    bound = LARGEST + RATE * LARGEST * LARGEST * tokens
    return 2.0 ** math.floor(math.log2(float(jnp.finfo(WIRE).max) / bound))


def on_device(params, inputs, cotangent, mix):
    weights = params[0]
    features = inputs[0]
    cot_local = cotangent[0]
    rows = weights.shape[0]
    shards = lax.axis_size("fsdp")
    scale = wire_scale(features.shape[0] * shards)
    replica = lax.axis_index("blk")
    shard = lax.axis_index("fsdp")
    row = lax.dynamic_slice_in_dim(mix, replica, 1, axis=0).astype(jnp.float32) / MIX_DENOM
    left, own, right = row[:, 0:1], row[:, 1:2], row[:, 2:3]
    even = replica % 2 == 0
    sides = [jnp.where(even, right, left) / scale, own, jnp.where(even, left, right) / scale]
    coeff = jnp.broadcast_to(jnp.concatenate(sides, axis=0), (3, weights.shape[1]))
    first = min(FIRST, rows // 2)
    main = rows - first
    cuts = list(range(0, main, STEP)) + [main]
    chunks = len(cuts) - 1

    def owner(away, shard=shard):
        other = shard + away
        return jnp.where(other < shards, other, other - shards)

    def partial(owner, start, size):
        block = lax.dynamic_slice_in_dim(features, owner * rows + start, size, axis=1)
        return lax.dot_general(
            block, cot_local, (((0,), (0,)), ((), ())), preferred_element_type=jnp.float32
        )

    def for_others(start, stop):
        return [
            (partial(owner(away), start, stop - start) * (RATE * scale)).astype(WIRE)
            for away in range(1, shards)
        ]

    def own_part(shard, start, stop):
        return weights[start:stop] - RATE * partial(shard, start, stop - start)

    def add_over_fsdp(terms):
        return [from_behind(term, "fsdp", away) for away, term in zip(range(1, shards), terms)]

    def u_of(chunk):
        start, stop = cuts[chunk], cuts[chunk + 1]
        total = base[0][start:stop] if stop <= split else base[1][start - split:stop - split]
        for term in arrived[chunk]:
            total = total - term.astype(jnp.float32) / scale
        return total

    def mixture(near, own, far):
        return (
            coeff[0:1] * near.astype(jnp.float32) + coeff[1:2] * own + coeff[2:3] * far.astype(jnp.float32)
        )

    def mix_into(out, chunk):
        value = mixture(near[chunk], u_of(chunk), far[chunk])
        return lax.dynamic_update_slice_in_dim(out, value, cuts[chunk], axis=0)

    near = {}
    far = {}
    mixed = 0
    out = jnp.zeros_like(weights)
    split = cuts[min(2, chunks)]
    terms = {0: for_others(0, cuts[1])}
    arrived = {0: add_over_fsdp(terms[0])}

    parts = [own_part(shard, main, rows)]
    parts += [-RATE * partial(owner(away), main, first) for away in range(1, shards)]
    parts = jnp.concatenate(parts, axis=0)
    parts, sent = lax.optimization_barrier((parts, (parts * scale).astype(WIRE)))
    far[-1] = swapped(sent, "blk", 1)
    near[-1] = swapped(sent, "blk", 0)

    if chunks > 1:
        parts, later = lax.optimization_barrier((parts, shard))
        rest = [
            (partial(owner(away, later), cuts[1], main - cuts[1]) * (RATE * scale)).astype(WIRE)
            for away in range(1, shards)
        ]
        for chunk in range(1, chunks):
            terms[chunk] = [term[cuts[chunk] - cuts[1]:cuts[chunk + 1] - cuts[1]] for term in rest]
        for chunk in range(1, min(AHEAD, chunks)):
            if chunk == 2:
                terms[chunk], near[-1] = lax.optimization_barrier((terms[chunk], near[-1]))
            arrived[chunk] = add_over_fsdp(terms[chunk])
    base = [own_part(shard, 0, split)]

    arrived[0], base, terms = lax.optimization_barrier((arrived[0], base, terms))
    for chunk in range(chunks):
        if chunk == 1:
            arrived[1], base = lax.optimization_barrier((arrived[1], base))
        if chunk >= 1:
            arrived[chunk], far[chunk - 2] = lax.optimization_barrier((arrived[chunk], far[chunk - 2]))
        arrived[chunk], near[chunk - 1] = lax.optimization_barrier((arrived[chunk], near[chunk - 1]))
        if mixed:
            arrived[chunk], out = lax.optimization_barrier((arrived[chunk], out))
        if chunk == 3:
            arrived[chunk], parts = lax.optimization_barrier((arrived[chunk], parts))
        sent = (u_of(chunk) * scale).astype(WIRE)
        sent, base, out, later = lax.optimization_barrier((sent, base, out, shard))
        if chunk == 0 and split < main:
            base.append(own_part(later, split, main))
        if chunk == min(1, chunks - 1):
            coeff, parts, sent = lax.optimization_barrier((coeff, parts, sent))
            parts = mixture(near[-1], parts, far[-1])
            back = [
                (parts[away * first:(away + 1) * first] * scale).astype(WIRE) for away in range(1, shards)
            ]
            parts = parts[:first]
        after = chunk + AHEAD
        if after < chunks:
            terms[after], sent = lax.optimization_barrier((terms[after], sent))
            arrived[after] = add_over_fsdp(terms[after])
        if after == max(chunks, AHEAD):
            back, sent = lax.optimization_barrier((back, sent))
            back = add_over_fsdp(back)
        far[chunk] = swapped(sent, "blk", 1)
        near[chunk] = swapped(sent, "blk", 0)
        if chunk >= MIXLAG:
            out = mix_into(out, mixed)
            mixed += 1

    for term in back:
        parts = parts + term.astype(jnp.float32) / scale
    out = lax.dynamic_update_slice_in_dim(out, parts, main, axis=0)
    for chunk in range(mixed, chunks):
        out = mix_into(out, chunk)
    return out[None]


def solution(mesh):
    return jax.shard_map(
        on_device,
        mesh=mesh,
        in_specs=(P("blk", "fsdp", None), P("blk", "fsdp", None), P("blk", "fsdp", None), P()),
        out_specs=P("blk", "fsdp", None),
        check_vma=False,
    )
```
